32 devices in a mesh: guide: 2 (over core), row: 4 (over z), col: 4 (over y, x).
Axes of the slice: x: 2, y: 2, z: 4, core: 2. Of those that a mesh axis runs over, the one named last changes fastest.
Arguments:
- hidden: bfloat16 [2, 16, 2048], P('guide', None, 'row')
- lengths: int32 [2, 16], P('guide'), may hold values from 2 to 512, as said below
- kv_cache: bfloat16 [2, 16, 2, 512, 512], P('guide', None, None, 'row', 'col'), as said below
- attn_gain: bfloat16 [2048], P('row'), may hold values from 0.5 to 1.5
- w_query: bfloat16 [2048, 2048], P('row', 'col'), may hold values from -0.125 to 0.125
- w_key_value: bfloat16 [2048, 2, 512], P('row', None, 'col'), may hold values from -0.125 to 0.125
- w_out: bfloat16 [2048, 2048], P('col', 'row'), may hold values from -0.125 to 0.125
- mlp_gain: bfloat16 [2048], P('row'), may hold values from 0.5 to 1.5
- w_gate_up: bfloat16 [2048, 2, 8192], P('row', None, 'col'), may hold values from -0.125 to 0.125
- w_down: bfloat16 [8192, 2048], P('col', 'row'), may hold values from -0.0625 to 0.0625
- final_gain: bfloat16 [2048], P('row'), may hold values from 0.5 to 1.5
- w_head: bfloat16 [2048, 128256], P('row', 'col'), may hold values from -0.1875 to 0.1875
- next_gain: bfloat16 [2048], P('row'), may hold values from 0.5 to 1.5
- w_next_query: bfloat16 [2048, 2048], P('row', 'col'), may hold values from -0.125 to 0.125
- w_next_kv: bfloat16 [2048, 2, 512], P('row', None, 'col'), may hold values from -0.125 to 0.125
- tenant: int32 [16], replicated, may hold values from 0 to 3
- guide_scale: float32 [4], replicated, may hold values from 1.5 to 6
Outputs:
- guided_logits: float32 [16, 128256], P('guide', ('col', 'row'))
- next_query: bfloat16 [2, 16, 2048], P('guide', None, 'col')
- next_key_value: bfloat16 [2, 16, 2, 512], P('guide', None, None, 'col')
The draws below stay inside these ranges and needn't reach their ends.
Inputs may be any that keep to these rules, and one draw needn't show every extreme that they name: `lengths`: in each group one request has exactly 512 cached positions. `kv_cache`: keys (index 0 of the third dimension) are stored with the rotary embedding of their positions; values at index 1.
All inputs are finite; a program needn't handle non-finite values.
Results may differ from the reference program's by a relative error of at most 0.013.
Values may be sent and summed in bfloat16 or wider, within the bound.
A program may use at most 128 MiB of HBM per device.

```python
import math
import jax
import jax.numpy as jnp
from jax import lax

D = 2048
HEADS = 32
KVH = 8
HD = 64
FF = 8192
V = 128256
REQ = 16
TENANTS = 4
QW = 2048
KVW = 512
MAXLEN = 512


def draw_hidden(key, part):
    full_shape = (2, REQ, D)
    drawn = jax.random.normal(key, full_shape, jnp.float32)
    column_ramp = jnp.exp(jnp.log(3.0) * jnp.arange(D, dtype=jnp.float32) / D)
    drawn = drawn * column_ramp
    return drawn.astype(jnp.bfloat16)


def draw_lengths(key, part):
    upper = jax.random.randint(jax.random.fold_in(key, 37), (2, REQ), 3, MAXLEN + 1)
    drawn = jax.random.randint(key, (2, REQ), 2, upper)
    longest = jax.random.randint(jax.random.fold_in(key, 31), (2, 1), 0, REQ)
    return jnp.where(jnp.arange(REQ)[None, :] == longest, MAXLEN, drawn).astype(jnp.int32)


def draw_kv_cache(key, part):
    full_shape = (2, REQ, 2, MAXLEN, KVW)
    which = jnp.arange(2).reshape(1, 1, 2, 1, 1)
    slot = jnp.arange(MAXLEN).reshape(1, 1, 1, MAXLEN, 1)
    spread = jnp.where(which == 0, 1.5, 1.0)
    common = jax.random.normal(jax.random.fold_in(key, 41), (2, REQ, 1, 1, KVW), jnp.float32)
    drawn = jax.random.normal(key, full_shape, jnp.float32) * spread
    ramp = 0.6 * jnp.exp(jnp.log(4.0) * slot.astype(jnp.float32) / MAXLEN)
    drawn = drawn + jnp.where(which == 1, ramp * common, 0.0)
    return drawn.astype(jnp.bfloat16)


def touch_ends(entries, key, smallest, top_value):
    extent = entries.shape
    place = [jax.random.randint(jax.random.fold_in(key, axis), (), 0, extent[axis]) for axis in range(len(extent))]
    entries = entries.at[tuple(place)].set(smallest)
    longest = extent.index(max(extent))
    place[longest] = (place[longest] + 1) % extent[longest]
    return entries.at[tuple(place)].set(top_value)


def raised(drawn, stream_key, source, target, parts, factor):
    owner, partner = [(jnp.arange(drawn.shape[axis_at]) // (drawn.shape[axis_at] // parts)).reshape([-1 if axis == axis_at else 1 for axis in range(drawn.ndim)]) for axis_at in (source, target)]
    chosen = jax.random.permutation(stream_key, parts)[partner]
    strong = (owner == chosen) | (owner == (partner + parts // 2) % parts)
    return jnp.where(strong, factor * drawn, drawn)


def block_levels(stream_key, extent, split, least, largest):
    def one(dim, shards_of):
        draws = jax.random.uniform(jax.random.fold_in(jax.random.fold_in(stream_key, 6), dim), (shards_of,), jnp.float32, least / len(split), largest / len(split))
        return jnp.repeat(jnp.exp(draws), extent[dim] // shards_of).reshape((-1,) + (1,) * (len(extent) - dim - 1))

    loudness = one(*split[0])
    for cut in split[1:]:
        loudness = loudness * one(*cut)
    return loudness


def gaussian(own_key, extent, deviation, limit, split=(), kind=jnp.bfloat16):
    factor_of = block_levels(own_key, extent, split, -0.22, 0.18) if split else 1.0
    drawn = jax.random.normal(own_key, extent, jnp.float32) * deviation * factor_of
    return jnp.minimum(jnp.maximum(drawn, -limit), limit).astype(kind)


def bell_draw_with(stream_key, shape, scale, most, pieces, heavy, held_as=jnp.bfloat16):
    drawn = scale * jax.random.normal(stream_key, shape, jnp.float32)
    if pieces:
        drawn = drawn * block_levels(stream_key, shape, pieces, -0.22, 0.18)
    return jnp.clip(raised(drawn, jax.random.fold_in(stream_key, 3), *heavy), -most, most).astype(held_as)


def setup_inputs(seed: int = 0) -> dict:
    keys = jax.random.split(jax.random.key(seed), 18)
    hidden = draw_hidden(jax.random.fold_in(keys[17], 71), 0)
    lengths = draw_lengths(jax.random.fold_in(keys[17], 71), 0)
    kv_cache = draw_kv_cache(jax.random.fold_in(keys[17], 71), 0)
    attn_gain = jnp.clip(1.0 + 0.1 * jax.random.normal(keys[3], (D,), jnp.float32), 0.5, 1.5).astype(jnp.bfloat16)
    w_query = gaussian(keys[4], (D, QW), D ** -0.5, 0.125, ((0, 4), (1, 4)))
    w_key_value = gaussian(keys[5], (D, 2, KVW), D ** -0.5, 0.125, ((0, 4), (2, 4)))
    w_out = gaussian(keys[6], (QW, D), QW ** -0.5, 0.125, ((0, 4), (1, 4)))
    mlp_gain = jnp.clip(1.0 + 0.1 * jax.random.normal(keys[7], (D,), jnp.float32), 0.5, 1.5).astype(jnp.bfloat16)
    w_gate_up = gaussian(keys[8], (D, 2, FF), D ** -0.5, 0.125, ((0, 4), (2, 4)))
    w_down = gaussian(keys[9], (FF, D), FF ** -0.5, 0.0625, ((0, 4), (1, 4)))
    final_gain = jnp.clip(1.0 + 0.1 * jax.random.normal(keys[10], (D,), jnp.float32), 0.5, 1.5).astype(jnp.bfloat16)
    w_head = bell_draw_with(keys[11], (D, V), D ** -0.5, 0.1875, ((0, 4), (1, 4)), (0, 1, 4, 2.0))
    next_gain = jnp.clip(1.0 + 0.1 * jax.random.normal(keys[12], (D,), jnp.float32), 0.5, 1.5).astype(jnp.bfloat16)
    w_next_query = gaussian(keys[13], (D, QW), D ** -0.5, 0.125, ((0, 4), (1, 4)))
    w_next_kv = gaussian(keys[14], (D, 2, KVW), D ** -0.5, 0.125, ((0, 4), (2, 4)))
    tenant = touch_ends(jax.random.randint(keys[15], (REQ,), 0, TENANTS), jax.random.fold_in(keys[15], 1), 0, TENANTS - 1).astype(jnp.int32)
    guide_scale = jnp.clip(jnp.exp(jax.random.uniform(keys[16], (TENANTS,), jnp.float32, math.log(1.5), math.log(6.0))), 1.5, 6.0)
    return dict(hidden=hidden, lengths=lengths, kv_cache=kv_cache, attn_gain=attn_gain, w_query=w_query, w_key_value=w_key_value, w_out=w_out, mlp_gain=mlp_gain, w_gate_up=w_gate_up, w_down=w_down, final_gain=final_gain, w_head=w_head, next_gain=next_gain, w_next_query=w_next_query, w_next_kv=w_next_kv, tenant=tenant, guide_scale=guide_scale)


EPSILON = 1e-05
ROPE_BASE = 500000.0
NEGATIVE = -1e+30

def rotate(vectors, position):
    half_width = vectors.shape[-1] // 2
    frequency = ROPE_BASE ** (-2.0 * jnp.arange(half_width, dtype=jnp.float32) / vectors.shape[-1])
    angles = position.astype(jnp.float32)[:, None] * frequency[None, :]
    angles = angles.reshape((angles.shape[0],) + (1,) * (vectors.ndim - 2) + (half_width,))
    cosine = jnp.cos(angles)
    sines = jnp.sin(angles)
    first_half = vectors[..., :half_width]
    second_half = vectors[..., half_width:]
    return jnp.concatenate([first_half * cosine - second_half * sines, second_half * cosine + first_half * sines], axis=-1)

def norm_scale(values):
    return lax.rsqrt(lax.optimization_barrier(jnp.mean(values * values, axis=-1, keepdims=True)) + EPSILON)

def group_pass(x_rows, length, cache_block, attn_gain, w_query, w_key_value, w_out, mlp_gain, w_gate_up, w_down, final_gain, w_head, next_gain, w_next_query, w_next_kv):
    requests = x_rows.shape[0]
    group_size = HEADS // KVH
    x_float = x_rows.astype(jnp.float32)
    scaling = norm_scale(x_float)
    normed = (x_float * attn_gain.astype(jnp.float32)).astype(jnp.bfloat16)
    query = scaling * jnp.dot(normed, w_query, preferred_element_type=jnp.float32)
    key_value = scaling * jnp.dot(normed, w_key_value.reshape(D, 2 * KVW), preferred_element_type=jnp.float32)
    query = rotate(query.reshape(requests, KVH, group_size, HD), length).astype(jnp.bfloat16)
    new_key = rotate(key_value[:, :KVW].reshape(requests, KVH, HD), length).astype(jnp.bfloat16)
    new_value = key_value[:, KVW:].reshape(requests, KVH, HD).astype(jnp.bfloat16)
    cache_keys = cache_block[:, 0].reshape(requests, MAXLEN, KVH, HD)
    cache_values = cache_block[:, 1].reshape(requests, MAXLEN, KVH, HD)
    inv_scale = HD ** (-0.5)
    scores = jnp.einsum('bhgd,bshd->bhgs', query.astype(jnp.float32), cache_keys.astype(jnp.float32)) * inv_scale
    own_score = jnp.einsum('bhgd,bhd->bhg', query.astype(jnp.float32), new_key.astype(jnp.float32)) * inv_scale
    usable = (jnp.arange(MAXLEN, dtype=jnp.int32)[None, :] < length[:, None])[:, None, None, :]
    masked = jnp.where(usable, scores, NEGATIVE)
    best = jnp.maximum(lax.optimization_barrier(jnp.max(masked, axis=-1)), own_score)
    exp_terms = jnp.where(usable, jnp.exp(masked - best[..., None]), 0.0)
    own_exp = jnp.exp(own_score - best)
    norm_sum = lax.optimization_barrier(jnp.sum(exp_terms, axis=-1)) + own_exp
    rounded = lax.optimization_barrier(exp_terms.astype(jnp.bfloat16)).astype(jnp.float32)
    own_rounded = lax.optimization_barrier(own_exp.astype(jnp.bfloat16)).astype(jnp.float32)
    weighted = jnp.einsum('bhgs,bshd->bhgd', rounded, cache_values.astype(jnp.float32))
    weighted = weighted + own_rounded[..., None] * new_value.astype(jnp.float32)[:, :, None, :]
    attended = (weighted / norm_sum[..., None]).reshape(requests, QW).astype(jnp.bfloat16)
    residual_one = (x_float + jnp.dot(attended, w_out, preferred_element_type=jnp.float32)).astype(jnp.bfloat16)
    one_float = residual_one.astype(jnp.float32)
    mlp_scale = norm_scale(one_float)
    mlp_input = (one_float * mlp_gain.astype(jnp.float32)).astype(jnp.bfloat16)
    gate_up = jnp.dot(mlp_input, w_gate_up.reshape(D, 2 * FF), preferred_element_type=jnp.float32)
    activation = (jax.nn.silu(mlp_scale * gate_up[:, :FF]) * (mlp_scale * gate_up[:, FF:])).astype(jnp.bfloat16)
    residual_two = (one_float + jnp.dot(activation, w_down, preferred_element_type=jnp.float32)).astype(jnp.bfloat16)
    two_float = residual_two.astype(jnp.float32)
    out_scale = norm_scale(two_float)
    head_input = (two_float * final_gain.astype(jnp.float32)).astype(jnp.bfloat16)
    next_input = (two_float * next_gain.astype(jnp.float32)).astype(jnp.bfloat16)
    group_logits = out_scale * jnp.dot(head_input, w_head, preferred_element_type=jnp.float32)
    next_query = (out_scale * jnp.dot(next_input, w_next_query, preferred_element_type=jnp.float32)).astype(jnp.bfloat16)
    next_pairs = (out_scale * jnp.dot(next_input, w_next_kv.reshape(D, 2 * KVW), preferred_element_type=jnp.float32)).astype(jnp.bfloat16)
    return (group_logits, next_query, next_pairs.reshape(requests, 2, KVW))

def reference(hidden, lengths, kv_cache, attn_gain, w_query, w_key_value, w_out, mlp_gain, w_gate_up, w_down, final_gain, w_head, next_gain, w_next_query, w_next_kv, tenant, guide_scale):
    results = []
    for which in range(2):
        results.append(group_pass(hidden[which], lengths[which], kv_cache[which], attn_gain, w_query, w_key_value, w_out, mlp_gain, w_gate_up, w_down, final_gain, w_head, next_gain, w_next_query, w_next_kv))
    guidance = lax.optimization_barrier(jnp.sum(jnp.where(tenant[:, None] == jnp.arange(TENANTS, dtype=jnp.int32)[None, :], guide_scale[None, :], 0.0), axis=1))
    conditional = results[0][0]
    unconditional = results[1][0]
    guided_logits = unconditional + guidance[:, None] * (conditional - unconditional)
    next_query = jnp.stack([results[0][1], results[1][1]])
    next_key_value = jnp.stack([results[0][2], results[1][2]])
    return (guided_logits, next_query, next_key_value)
```

```python
import functools
import math

import jax
import jax.numpy as jnp
from jax import lax
from jax.experimental import pallas as pl
from jax.experimental.pallas import tpu as pltpu
from jax.sharding import PartitionSpec as P

D = 2048
HEADS = 32
KVH = 8
HD = 64
TENANTS = 4
EPSILON = 1e-05
ROPE_BASE = 500000.0
NEGATIVE = -1e30
LANES = 128
SUBLANES = 16
F32 = jnp.float32
BF16 = jnp.bfloat16
MESH = pl.DeviceIdType.MESH


def mm(a, b):
    return jnp.dot(a, b, preferred_element_type=F32)


def iota(shape, dim):
    return lax.broadcasted_iota(jnp.int32, shape, dim)


def window_of(block):
    tiles = -(-(block + LANES - 1) // LANES)
    return (tiles + tiles % 2) * LANES


def layer_kernel(
    n,
    m,
    x_ref,
    len_ref,
    tenant_ref,
    guide_ref,
    gains_ref,
    kv_hbm,
    wq_hbm,
    wkv_hbm,
    wo_hbm,
    wgu_hbm,
    wd_hbm,
    wh_hbm,
    wnq_hbm,
    wnkv_hbm,
    out_ref,
    nq_ref,
    nkv_ref,
    kv,
    wq,
    wkv,
    wo,
    wgu,
    wd,
    wh,
    wnq,
    wnkv,
    q_buf,
    sq_buf,
    q_rows,
    a_buf,
    o_buf,
    sq2_buf,
    gu_send,
    gu_buf,
    act_buf,
    d_buf,
    two_buf,
    sq3_buf,
    np_buf,
    part,
    h_send,
    h_buf,
    local_sem,
    send_sem,
    recv_sem,
):
    row = lax.axis_index("row")
    col = lax.axis_index("col")
    guide = lax.axis_index("guide")
    place = {"row": (row, n), "col": (col, m), "guide": (guide, 2)}

    pairs = [
        (wq_hbm, wq),
        (wkv_hbm, wkv),
        (kv_hbm, kv),
        (wo_hbm, wo),
        (wgu_hbm, wgu),
        (wd_hbm, wd),
        (wnq_hbm, wnq),
        (wnkv_hbm, wnkv),
        (wh_hbm, wh),
    ]
    loads = [pltpu.make_async_copy(a, b, local_sem.at[i]) for i, (a, b) in enumerate(pairs)]
    for load in loads:
        load.start()

    def peer(axis, k):
        me, size = place[axis]
        return lax.rem(me + k, size)

    barrier = pltpu.get_barrier_semaphore()
    for axis in ("row", "col", "guide"):
        for k in range(1, place[axis][1]):
            pl.semaphore_signal(barrier, inc=1, device_id={axis: peer(axis, k)}, device_id_type=MESH)

    def send(source, target, axis, number, k):
        copy = pltpu.make_async_remote_copy(
            src_ref=source,
            dst_ref=target,
            send_sem=send_sem.at[number, k - 1],
            recv_sem=recv_sem.at[number, k - 1],
            device_id={axis: peer(axis, k)},
            device_id_type=MESH,
        )
        copy.start()
        return copy

    def spread(buf, axis, number):
        me, size = place[axis]
        return [send(buf.at[me], buf.at[me], axis, number, k) for k in range(1, size)]

    def finish(copies):
        for copy in copies:
            copy.wait()

    def total(buf, size):
        result = buf[0].astype(F32)
        for k in range(1, size):
            result = result + buf[k].astype(F32)
        return result

    def squares(values):
        return jnp.broadcast_to(jnp.sum(values * values, axis=1, keepdims=True), (values.shape[0], LANES))

    def scale_of(sums):
        return lax.rsqrt(sums / D + EPSILON)

    requests = x_ref.shape[0]
    half_rows = requests // 2
    x_float = x_ref[...].astype(F32)
    normed = (x_float * gains_ref[0:1, :]).astype(BF16)
    sq_buf[row] = squares(x_float)
    loads[0].wait()
    width_q = wq.shape[1]
    width_kv = wkv.shape[1]
    q_buf[row, :, 0:width_q] = mm(normed, wq[...]).astype(BF16)
    loads[1].wait()
    q_buf[row, :, width_q : width_q + width_kv] = mm(normed, wkv[...]).astype(BF16)
    pl.semaphore_wait(barrier, n - 1 + m - 1 + 1)
    copies = spread(sq_buf, "row", 0) + spread(q_buf, "row", 1)

    lane = iota((requests, LANES), 1)
    lengths_row = len_ref[...].astype(F32)
    pick = iota((requests, requests), 0) == iota((requests, requests), 1)
    length_col = jnp.sum(jnp.where(pick, lengths_row, 0.0), axis=1, keepdims=True)
    frequency = jnp.exp((lane % (HD // 2)).astype(F32) * (-2.0 * math.log(ROPE_BASE) / HD))
    angles = length_col * frequency
    cosine = jnp.cos(angles)
    sine = jnp.sin(angles)
    low = (lane % HD) < HD // 2
    signed = jnp.where(low, -sine, sine)
    left = lane < HD

    def rotated(tile):
        ahead = pltpu.roll(tile, LANES - HD // 2, 1)
        behind = pltpu.roll(tile, HD // 2, 1)
        return tile * cosine + jnp.where(low, ahead, behind) * signed

    finish(copies)
    scale = scale_of(total(sq_buf, n))
    sums = total(q_buf, n)
    tiles = [scale * sums[:, t * LANES : (t + 1) * LANES] for t in range((width_q + width_kv) // LANES)]
    q_tiles = width_q // LANES
    heads_here = 2 * q_tiles
    group = HEADS // KVH
    for t in range(q_tiles):
        tile = rotated(tiles[t]).astype(BF16).astype(F32)
        swapped = pltpu.roll(tile, HD, 1)
        for side in range(2):
            j = 2 * t + side
            kv_head = j // group
            wanted = tile if side == kv_head else swapped
            q_rows[:, j, :] = jnp.where(left == (kv_head == 0), wanted, 0.0)
    new_key = rotated(tiles[q_tiles]).astype(BF16).astype(F32)
    new_value = tiles[q_tiles + 1].astype(BF16).astype(F32)

    loads[2].wait()
    inv_scale = HD**-0.5
    span = kv.shape[2]
    rows3 = (requests, heads_here, LANES)
    q3 = q_rows[...]
    scores = jnp.stack(
        [
            lax.dot_general(
                q3[b].astype(BF16), kv[b, 0], (((1,), (1,)), ((), ())), preferred_element_type=F32
            )
            for b in range(requests)
        ]
    ) * inv_scale
    own_score = jnp.sum(q3 * new_key[:, None, :], axis=2, keepdims=True) * inv_scale
    length3 = length_col[:, :, None]
    position = (row * span + iota((requests, heads_here, span), 2)).astype(F32)
    usable = position < length3
    masked = jnp.where(usable, scores, NEGATIVE)
    best = jnp.max(masked, axis=2, keepdims=True)
    terms = jnp.where(usable, jnp.exp(masked - best), 0.0)
    norm = jnp.sum(terms, axis=2, keepdims=True)
    weighted = jnp.stack([mm(terms[b].astype(BF16), kv[b, 1]) for b in range(requests)])
    lane3 = iota(rows3, 2)
    mine = (lane3 < HD) == (iota(rows3, 1) < group)
    is_best = jnp.logical_and(jnp.logical_not(mine), lane3 % HD < HD // 2)
    is_norm = jnp.logical_and(jnp.logical_not(mine), lane3 % HD >= HD // 2)
    a_buf[row] = jnp.where(mine, weighted, jnp.where(is_best, best, norm))
    copies = spread(a_buf, "row", 2)
    finish(copies)
    bests = [
        jnp.max(jnp.where(is_best, a_buf[k], -3e38), axis=2, keepdims=True) for k in range(n)
    ]
    final_best = own_score
    for value in bests:
        final_best = jnp.maximum(final_best, value)
    own_exp = jnp.exp(own_score - final_best)
    norm_sum = own_exp
    attended = own_exp.astype(BF16).astype(F32) * new_value[:, None, :]
    for k in range(n):
        factor = jnp.exp(bests[k] - final_best)
        message = a_buf[k]
        norm_k = jnp.max(jnp.where(is_norm, message, 0.0), axis=2, keepdims=True)
        norm_sum = norm_sum + norm_k * factor
        attended = attended + message * factor
    q_rows[...] = attended / norm_sum
    att_tiles = []
    for t in range(q_tiles):
        even = q_rows[:, 2 * t, :]
        odd = q_rows[:, 2 * t + 1, :]
        if 2 * t < group:
            att_tiles.append(jnp.where(left, even, pltpu.roll(odd, HD, 1)))
        else:
            att_tiles.append(jnp.where(left, pltpu.roll(even, HD, 1), odd))
    attended2 = jnp.concatenate(att_tiles, axis=1).astype(BF16)

    loads[3].wait()
    o_buf[col] = mm(attended2, wo[...]).astype(BF16)
    finish(spread(o_buf, "col", 3))
    one_float = (x_float + total(o_buf, m)).astype(BF16).astype(F32)

    sq2_buf[row] = squares(one_float)
    sq_copies = spread(sq2_buf, "row", 4)
    mlp_input = (one_float * gains_ref[1:2, :]).astype(BF16)
    loads[4].wait()
    hidden_here = wgu.shape[1] // 2
    block = hidden_here // n
    if block % LANES == 0:
        copies = []
        for k in range(1, n + 1):
            dest = peer("row", k)
            start = pl.multiple_of(dest * block, LANES)
            gate = mm(mlp_input, wgu[:, pl.ds(start, block)])
            up = mm(mlp_input, wgu[:, pl.ds(hidden_here + start, block)])
            joined = jnp.concatenate([gate, up], axis=1).astype(BF16)
            if k < n:
                gu_send[k - 1] = joined
                copies.append(send(gu_send.at[k - 1], gu_buf.at[row], "row", 5, k))
            else:
                gu_buf[row] = joined
        finish(sq_copies)
        mlp_scale = scale_of(total(sq2_buf, n))[:, 0:1]
        finish(copies)
        sums = total(gu_buf, n) * mlp_scale
        gate, up = sums[:, :block], sums[:, block:]
        act_buf[row] = (gate / (1.0 + jnp.exp(-gate)) * up).astype(BF16)
        finish(spread(act_buf, "row", 6))
        loads[5].wait()
        down = mm(act_buf[0], wd[0:block, :])
        for k in range(1, n):
            down = down + mm(act_buf[k], wd[k * block : (k + 1) * block, :])
    else:
        gu_buf[row] = mm(mlp_input, wgu[...]).astype(BF16)
        copies = spread(gu_buf, "row", 5)
        finish(sq_copies)
        mlp_scale = scale_of(total(sq2_buf, n))[:, 0:1]
        finish(copies)
        sums = total(gu_buf, n) * mlp_scale
        gate, up = sums[:, :hidden_here], sums[:, hidden_here:]
        loads[5].wait()
        down = mm((gate / (1.0 + jnp.exp(-gate)) * up).astype(BF16), wd[...])
    d_buf[col] = down.astype(BF16)
    finish(spread(d_buf, "col", 7))
    two_own = (one_float + total(d_buf, m)).astype(BF16)

    two_buf[guide] = two_own
    two_copies = spread(two_buf, "guide", 8)
    own_float = two_own.astype(F32)
    next_input = (own_float * gains_ref[3:4, :]).astype(BF16)
    loads[6].wait()
    np_buf[row, :, 0:width_q] = mm(next_input, wnq[...]).astype(BF16)
    loads[7].wait()
    np_buf[row, :, width_q : width_q + width_kv] = mm(next_input, wnkv[...]).astype(BF16)
    finish(two_copies)
    first = guide == 0

    def my_half(values):
        return jnp.where(first, values[:half_rows], values[half_rows:])

    both = jnp.concatenate(
        [my_half(two_buf[0].astype(F32)), my_half(two_buf[1].astype(F32))], axis=0
    )
    sq3_buf[row] = jnp.where(left, squares(own_float), squares(both))
    sq_copies = spread(sq3_buf, "row", 9)
    np_copies = spread(np_buf, "row", 10)
    head_input = (both * gains_ref[2:3, :]).astype(BF16)

    guidance_row = jnp.zeros((1, requests), F32)
    for k in range(TENANTS):
        guidance_row = guidance_row + jnp.where(tenant_ref[...] == k, guide_ref[k], 0.0)
    here = iota((half_rows, requests), 1) == iota((half_rows, requests), 0) + guide * half_rows
    guidance = jnp.sum(jnp.where(here, guidance_row, 0.0), axis=1, keepdims=True)

    finish(sq_copies)
    scales = scale_of(total(sq3_buf, n))
    own_scale = scales[:, 0:1]
    both_scale = scales[:, LANES - 1 : LANES]
    factor_c = guidance * both_scale[:half_rows]
    factor_u = (1.0 - guidance) * both_scale[half_rows:]

    def guided(rows):
        logits = lax.dot_general(
            head_input, rows, (((1,), (1,)), ((), ())), preferred_element_type=F32
        )
        return factor_c * logits[:half_rows] + factor_u * logits[half_rows:]

    loads[8].wait()
    vocab = wh.shape[0]
    share = vocab // n
    exact = share % SUBLANES == 0
    window = window_of(share)
    half = window // 2
    chunk = 1024 if half % 1024 == 0 else half
    whole = vocab // LANES * LANES
    last_start = (n - 1) * share // LANES * LANES
    copies = []
    if exact:
        part[...] = jnp.zeros(part.shape, F32)
    else:
        part[:, whole : part.shape[1]] = jnp.zeros((half_rows, part.shape[1] - whole), F32)
        if whole < vocab:
            part[:, whole:vocab] = guided(wh[whole:vocab, :])
    for k in range(1, n + 1):
        dest = peer("row", k)
        if exact:
            for piece in range(-(-share // chunk)):
                first_row = piece * chunk
                size = min(chunk, share - first_row)
                at = pl.multiple_of(dest * share + first_row, SUBLANES)
                top = first_row // half * half_rows
                column = first_row % half
                part[top : top + half_rows, column : column + size] = guided(wh[pl.ds(at, size), :])
            stacked = part[...]
        else:
            start = dest * share // LANES * LANES
            is_last = (dest + 1) // n
            for piece in range(window // chunk):
                over = max(0, last_start + (piece + 1) * chunk - whole)
                at = pl.multiple_of(start + piece * chunk - is_last * over, LANES)
                part[:, pl.ds(at, chunk)] = guided(wh[pl.ds(at, chunk), :])
            start = pl.multiple_of(start, LANES)
            upper = pl.multiple_of(start + half, LANES)
            stacked = jnp.concatenate(
                [part[:, pl.ds(start, half)], part[:, pl.ds(upper, half)]], axis=0
            )
        if k < n:
            h_send[k - 1] = stacked.astype(BF16)
            copies.append(send(h_send.at[k - 1], h_buf.at[row], "row", 11, k))
        else:
            h_buf[row] = stacked.astype(BF16)

    finish(np_copies)
    sums = own_scale * total(np_buf, n)
    nq_ref[...] = sums[:, :width_q].astype(BF16)
    nkv_ref[...] = sums[:, width_q:].astype(BF16)

    finish(copies)
    sums = total(h_buf, n)
    if exact:
        out_ref[:, 0:half] = sums[:half_rows]
        out_ref[:, half:share] = sums[half_rows:, 0 : share - half]
    else:
        part[:, 0:half] = sums[:half_rows]
        part[:, half:window] = sums[half_rows:]
        offset = lax.rem(row * share, LANES)
        turn = lax.rem(LANES - offset, LANES)
        lane8 = iota((half_rows, LANES), 1)
        for j in range(-(-share // LANES)):
            here_tile = pltpu.roll(part[:, j * LANES : (j + 1) * LANES], turn, 1)
            next_tile = pltpu.roll(part[:, (j + 1) * LANES : (j + 2) * LANES], turn, 1)
            joined = jnp.where(lane8 < LANES - offset, here_tile, next_tile)
            wide = min(LANES, share - j * LANES)
            out_ref[:, j * LANES : j * LANES + wide] = joined[:, :wide]


def local(
    n,
    m,
    hidden,
    lengths,
    kv_cache,
    attn_gain,
    w_query,
    w_key_value,
    w_out,
    mlp_gain,
    w_gate_up,
    w_down,
    final_gain,
    w_head,
    next_gain,
    w_next_query,
    w_next_kv,
    tenant,
    guide_scale,
):
    x_rows = hidden[0]
    requests, width = x_rows.shape
    gains = jnp.stack([attn_gain, mlp_gain, final_gain, next_gain]).astype(F32)
    w_kv = w_key_value.reshape(width, -1)
    w_gu = w_gate_up.reshape(width, -1)
    w_nkv = w_next_kv.reshape(width, -1)
    cache = kv_cache[0]
    head_rows = w_head.T
    weights = (cache, w_query, w_kv, w_out, w_gu, w_down, head_rows, w_next_query, w_nkv)
    width_q = w_query.shape[1]
    width_kv = w_kv.shape[1]
    heads_here = width_q // HD
    hidden_here = w_down.shape[0]
    block = hidden_here // n
    vocab = head_rows.shape[0]
    share = vocab // n
    window = window_of(share)
    last_start = (n - 1) * share // LANES * LANES
    exact = share % SUBLANES == 0
    part_shape = (requests, window // 2) if exact else (requests // 2, last_start + window)
    scattered = block % LANES == 0
    gu_width = 2 * block if scattered else 2 * hidden_here
    peers = max(n, m) - 1
    vmem = pl.BlockSpec(memory_space=pltpu.VMEM)
    smem = pl.BlockSpec(memory_space=pltpu.SMEM)
    hbm = pl.BlockSpec(memory_space=pl.ANY)
    scratch = [pltpu.VMEM(a.shape, a.dtype) for a in weights] + [
        pltpu.VMEM((n, requests, width_q + width_kv), BF16),
        pltpu.VMEM((n, requests, LANES), F32),
        pltpu.VMEM((requests, heads_here, LANES), F32),
        pltpu.VMEM((n, requests, heads_here, LANES), F32),
        pltpu.VMEM((m, requests, width), BF16),
        pltpu.VMEM((n, requests, LANES), F32),
        pltpu.VMEM((n - 1 if scattered else 1, requests, gu_width), BF16),
        pltpu.VMEM((n, requests, gu_width), BF16),
        pltpu.VMEM((n, requests, block), BF16),
        pltpu.VMEM((m, requests, width), BF16),
        pltpu.VMEM((2, requests, width), BF16),
        pltpu.VMEM((n, requests, LANES), F32),
        pltpu.VMEM((n, requests, width_q + width_kv), BF16),
        pltpu.VMEM(part_shape, F32),
        pltpu.VMEM((n - 1, requests, window // 2), BF16),
        pltpu.VMEM((n, requests, window // 2), BF16),
        pltpu.SemaphoreType.DMA((9,)),
        pltpu.SemaphoreType.DMA((12, peers)),
        pltpu.SemaphoreType.DMA((12, peers)),
    ]
    guided, next_query, next_pairs = pl.pallas_call(
        functools.partial(layer_kernel, n, m),
        out_shape=(
            jax.ShapeDtypeStruct((requests // 2, share), F32),
            jax.ShapeDtypeStruct((requests, width_q), BF16),
            jax.ShapeDtypeStruct((requests, width_kv), BF16),
        ),
        in_specs=[vmem, vmem, vmem, smem, vmem] + [hbm] * 9,
        out_specs=(vmem, vmem, vmem),
        scratch_shapes=scratch,
        compiler_params=pltpu.CompilerParams(
            collective_id=0, has_side_effects=True, vmem_limit_bytes=60 * 1024 * 1024
        ),
        name="decode_layer",
    )(x_rows, lengths, tenant.reshape(1, -1), guide_scale, gains, *weights)
    return (guided, next_query[None], next_pairs.reshape(1, requests, 2, -1))


def solution(mesh):
    placed = (
        P("guide", None, "row"),
        P("guide", None),
        P("guide", None, None, "row", "col"),
        P("row"),
        P("row", "col"),
        P("row", None, "col"),
        P("col", "row"),
        P("row"),
        P("row", None, "col"),
        P("col", "row"),
        P("row"),
        P("row", "col"),
        P("row"),
        P("row", "col"),
        P("row", None, "col"),
        P(),
        P(),
    )
    return jax.shard_map(
        functools.partial(local, mesh.shape["row"], mesh.shape["col"]),
        mesh=mesh,
        in_specs=placed,
        out_specs=(
            P("guide", ("col", "row")),
            P("guide", None, "col"),
            P("guide", None, None, "col"),
        ),
        check_vma=False,
    )
```

```python
import functools
import math

import jax
import jax.numpy as jnp
from jax import lax
from jax.experimental import pallas as pl
from jax.experimental.pallas import tpu as pltpu
from jax.sharding import PartitionSpec as P

D = 2048
HEADS = 32
KVH = 8
HD = 64
TENANTS = 4
EPSILON = 1e-05
ROPE_BASE = 500000.0
NEGATIVE = -1e30
LANES = 128
SUBLANES = 16
F32 = jnp.float32
BF16 = jnp.bfloat16
MESH = pl.DeviceIdType.MESH


def mm(a, b):
    return jnp.dot(a, b, preferred_element_type=F32)


def iota(shape, dim):
    return lax.broadcasted_iota(jnp.int32, shape, dim)


def window_of(block):
    tiles = -(-(block + LANES - 1) // LANES)
    return (tiles + tiles % 2) * LANES


def layer_kernel(
    n,
    m,
    x_ref,
    len_ref,
    tenant_ref,
    guide_ref,
    attn_gain_ref,
    mlp_gain_ref,
    final_gain_ref,
    next_gain_ref,
    kv_hbm,
    wq_hbm,
    wkv_hbm,
    wo_hbm,
    wgu_hbm,
    wd_hbm,
    wh_hbm,
    wnq_hbm,
    wnkv_hbm,
    out_ref,
    nq_ref,
    nkv_ref,
    kv,
    wq,
    wkv,
    wo,
    wgu,
    wd,
    wh,
    wnq,
    wnkv,
    weaver,
    q_buf,
    sq_buf,
    q_rows,
    stat_buf,
    a_buf,
    o_buf,
    sq2_buf,
    gu_send,
    gu_buf,
    act_buf,
    d_buf,
    two_buf,
    sq3_buf,
    np_buf,
    first_part,
    part,
    h_send,
    h_buf,
    local_sem,
    send_sem,
    recv_sem,
    sq_sem,
):
    row = lax.axis_index("row")
    col = lax.axis_index("col")
    guide = lax.axis_index("guide")
    place = {"row": (row, n), "col": (col, m), "guide": (guide, 2)}

    pairs = [
        (wq_hbm, wq),
        (wkv_hbm, wkv),
        (kv_hbm, kv),
        (wo_hbm, wo),
        (wgu_hbm, wgu),
        (wd_hbm, wd),
        (wnq_hbm, wnq),
        (wnkv_hbm, wnkv),
    ]
    loads = [pltpu.make_async_copy(a, b, local_sem.at[i]) for i, (a, b) in enumerate(pairs)]
    for load in loads:
        load.start()
    share = wh.shape[0] // n
    exact = share % SUBLANES == 0
    if exact:
        head_loads = []
        for k in range(1, n + 1):
            at = pl.ds(pl.multiple_of(lax.rem(row + k, n) * share, SUBLANES), share)
            head_loads.append(
                pltpu.make_async_copy(wh_hbm.at[at, :], wh.at[at, :], local_sem.at[7 + k])
            )
    else:
        head_loads = [pltpu.make_async_copy(wh_hbm, wh, local_sem.at[8])]
    early = (len(head_loads) + 1) // 2

    pending = []

    def peer(axis, k):
        me, size = place[axis]
        return lax.rem(me + k, size)

    other = 1 - guide
    barrier = pltpu.get_barrier_semaphore()
    for k in range(1, n):
        target = {"row": peer("row", k), "guide": other}
        pl.semaphore_signal(barrier, inc=1, device_id=target, device_id_type=MESH)
    for axis in ("row", "col", "guide"):
        for k in range(1, place[axis][1]):
            pl.semaphore_signal(barrier, inc=1, device_id={axis: peer(axis, k)}, device_id_type=MESH)

    def send(source, target, axis, number, k):
        copy = pltpu.make_async_remote_copy(
            src_ref=source,
            dst_ref=target,
            send_sem=send_sem.at[number, k - 1],
            recv_sem=recv_sem.at[number, k - 1],
            device_id={axis: peer(axis, k)},
            device_id_type=MESH,
        )
        copy.start()
        return copy

    def spread(buf, axis, number):
        me, size = place[axis]
        return [send(buf.at[me], buf.at[me], axis, number, k) for k in range(1, size)]

    def finish(copies):
        for copy in copies:
            copy.wait_recv()
            pending.append(copy)

    def total(buf, size):
        result = buf[0].astype(F32)
        for k in range(1, size):
            result = result + buf[k].astype(F32)
        return result

    def squares(values):
        return jnp.broadcast_to(jnp.sum(values * values, axis=1, keepdims=True), (values.shape[0], LANES))

    def scale_of(sums):
        return lax.rsqrt(sums / D + EPSILON)

    requests = x_ref.shape[0]
    depth = wgu.shape[0]
    width_q = wq.shape[1]
    key_width = wkv.shape[2]
    width_kv = 2 * key_width
    weaver[...] = (iota((depth, 2 * depth), 1) == 2 * iota((depth, 2 * depth), 0)).astype(BF16)

    def weave(values):
        even = mm(values, weaver[...])
        return jnp.concatenate([even, pltpu.roll(even, 1, 1)], axis=0).astype(BF16)

    def pairs_to(buf, values, weights):
        both_parts = mm(weave(values), weights[...].reshape(2 * depth, weights.shape[2]))
        buf[row, :, width_q : width_q + key_width] = both_parts[:requests].astype(BF16)
        buf[row, :, width_q + key_width : width_q + width_kv] = both_parts[requests:].astype(BF16)

    half_rows = requests // 2
    x_float = x_ref[...].astype(F32)
    normed = (x_float * attn_gain_ref[...].astype(F32)[None, :]).astype(BF16)
    sq_buf[row] = squares(x_float)
    loads[0].wait()
    q_buf[row, :, 0:width_q] = mm(normed, wq[...]).astype(BF16)
    loads[1].wait()
    pairs_to(q_buf, normed, wkv)
    pl.semaphore_wait(barrier, 2 * (n - 1) + m - 1 + 1)
    copies = spread(sq_buf, "row", 0) + spread(q_buf, "row", 1)
    for load in head_loads[:early]:
        load.start()

    lane = iota((requests, LANES), 1)
    lengths_row = len_ref[...].astype(F32)
    pick = iota((requests, requests), 0) == iota((requests, requests), 1)
    length_col = jnp.sum(jnp.where(pick, lengths_row, 0.0), axis=1, keepdims=True)
    frequency = jnp.exp((lane % (HD // 2)).astype(F32) * (-2.0 * math.log(ROPE_BASE) / HD))
    angles = length_col * frequency
    cosine = jnp.cos(angles)
    sine = jnp.sin(angles)
    low = (lane % HD) < HD // 2
    signed = jnp.where(low, -sine, sine)
    left = lane < HD

    def rotated(tile):
        ahead = pltpu.roll(tile, LANES - HD // 2, 1)
        behind = pltpu.roll(tile, HD // 2, 1)
        return tile * cosine + jnp.where(low, ahead, behind) * signed

    finish(copies)
    scale = scale_of(total(sq_buf, n))
    sums = total(q_buf, n)
    tiles = [scale * sums[:, t * LANES : (t + 1) * LANES] for t in range((width_q + width_kv) // LANES)]
    q_tiles = width_q // LANES
    heads_here = 2 * q_tiles
    group = HEADS // KVH
    for t in range(q_tiles):
        tile = rotated(tiles[t]).astype(BF16).astype(F32)
        swapped = pltpu.roll(tile, HD, 1)
        for side in range(2):
            j = 2 * t + side
            kv_head = j // group
            wanted = tile if side == kv_head else swapped
            q_rows[:, j, :] = jnp.where(left == (kv_head == 0), wanted, 0.0)
    new_key = rotated(tiles[q_tiles]).astype(BF16).astype(F32)
    new_value = tiles[q_tiles + 1].astype(BF16).astype(F32)

    loads[2].wait()
    inv_scale = HD**-0.5
    span = kv.shape[2]
    rows3 = (requests, heads_here, LANES)
    q3 = q_rows[...]
    scores = jnp.stack(
        [
            lax.dot_general(
                q3[b].astype(BF16), kv[b, 0], (((1,), (1,)), ((), ())), preferred_element_type=F32
            )
            for b in range(requests)
        ]
    ) * inv_scale
    own_score = jnp.sum(q3 * new_key[:, None, :], axis=2, keepdims=True) * inv_scale
    length3 = length_col[:, :, None]
    position = (row * span + iota((requests, heads_here, span), 2)).astype(F32)
    usable = position < length3
    masked = jnp.where(usable, scores, NEGATIVE)
    best = jnp.max(masked, axis=2, keepdims=True)
    terms = jnp.where(usable, jnp.exp(masked - best), 0.0)
    norm = jnp.sum(terms, axis=2, keepdims=True)
    weighted = jnp.stack([mm(terms[b].astype(BF16), kv[b, 1]) for b in range(requests)])
    lane3 = iota(rows3, 2)
    q_rows[...] = weighted

    def to_lanes(column):
        return jnp.sum(jnp.where(lane3 == iota(rows3, 1), column, 0.0), axis=1)

    def by_head(table, t):
        return jnp.where(left, table[:, 2 * t : 2 * t + 1], table[:, 2 * t + 1 : 2 * t + 2])

    stat_buf[row] = jnp.where(left, to_lanes(best), pltpu.roll(to_lanes(norm), HD, 1))
    for t in range(q_tiles):
        even = q_rows[:, 2 * t, :]
        odd = q_rows[:, 2 * t + 1, :]
        if 2 * t < group:
            tile = jnp.where(left, even, pltpu.roll(odd, HD, 1))
        else:
            tile = jnp.where(left, pltpu.roll(even, HD, 1), odd)
        a_buf[row, :, t * LANES : (t + 1) * LANES] = tile.astype(BF16)
    copies = spread(stat_buf, "row", 12) + spread(a_buf, "row", 2)
    for load in head_loads[early:]:
        load.start()
    own_lanes = to_lanes(own_score)
    turned_value = pltpu.roll(new_value, HD, 1)
    value_of = (jnp.where(left, new_value, turned_value), jnp.where(left, turned_value, new_value))
    finish(copies)
    bests = [stat_buf[k] for k in range(n)]
    final_best = own_lanes
    for value in bests:
        final_best = jnp.maximum(final_best, value)
    own_exp = jnp.exp(own_lanes - final_best)
    factors = [jnp.exp(value - final_best) for value in bests]
    norm_sum = own_exp
    for k in range(n):
        norm_sum = norm_sum + pltpu.roll(bests[k], HD, 1) * factors[k]
    own_factor = own_exp.astype(BF16).astype(F32)
    att_tiles = []
    for t in range(q_tiles):
        tile = by_head(own_factor, t) * value_of[2 * t // group]
        for k in range(n):
            tile = tile + by_head(factors[k], t) * a_buf[k, :, t * LANES : (t + 1) * LANES].astype(F32)
        att_tiles.append(tile / by_head(norm_sum, t))
    attended2 = jnp.concatenate(att_tiles, axis=1).astype(BF16)

    loads[3].wait()
    o_buf[col] = mm(attended2, wo[...]).astype(BF16)
    finish(spread(o_buf, "col", 3))
    one_float = (x_float + total(o_buf, m)).astype(BF16).astype(F32)

    sq2_buf[row] = squares(one_float)
    sq_copies = spread(sq2_buf, "row", 4)
    mlp_input = (one_float * mlp_gain_ref[...].astype(F32)[None, :]).astype(BF16)
    loads[4].wait()
    hidden_here = wgu.shape[2]
    block = hidden_here // n
    woven = weave(mlp_input)
    if block % LANES == 0:
        copies = []
        for k in range(1, n + 1):
            dest = peer("row", k)
            start = pl.multiple_of(dest * block, LANES)
            rows = wgu[:, :, pl.ds(start, block)].reshape(2 * wgu.shape[0], block)
            both_parts = mm(woven, rows)
            joined = jnp.concatenate([both_parts[:requests], both_parts[requests:]], axis=1).astype(BF16)
            if k < n:
                gu_send[k - 1] = joined
                copies.append(send(gu_send.at[k - 1], gu_buf.at[row], "row", 5, k))
            else:
                gu_buf[row] = joined
        finish(sq_copies)
        mlp_scale = scale_of(total(sq2_buf, n))[:, 0:1]
        finish(copies)
        sums = total(gu_buf, n) * mlp_scale
        gate, up = sums[:, :block], sums[:, block:]
        act_buf[row] = (gate / (1.0 + jnp.exp(-gate)) * up).astype(BF16)
        finish(spread(act_buf, "row", 6))
        loads[5].wait()
        down = mm(act_buf[0], wd[0:block, :])
        for k in range(1, n):
            down = down + mm(act_buf[k], wd[k * block : (k + 1) * block, :])
    else:
        both_parts = mm(woven, wgu[...].reshape(2 * wgu.shape[0], hidden_here))
        gu_buf[row, :, 0:hidden_here] = both_parts[:requests].astype(BF16)
        gu_buf[row, :, hidden_here : 2 * hidden_here] = both_parts[requests:].astype(BF16)
        copies = spread(gu_buf, "row", 5)
        finish(sq_copies)
        mlp_scale = scale_of(total(sq2_buf, n))[:, 0:1]
        finish(copies)
        sums = total(gu_buf, n) * mlp_scale
        gate, up = sums[:, :hidden_here], sums[:, hidden_here:]
        loads[5].wait()
        down = mm((gate / (1.0 + jnp.exp(-gate)) * up).astype(BF16), wd[...])
    d_buf[col] = down.astype(BF16)
    finish(spread(d_buf, "col", 7))
    two_own = (one_float + total(d_buf, m)).astype(BF16)

    two_buf[guide] = two_own
    two_copies = spread(two_buf, "guide", 8)
    own_float = two_own.astype(F32)
    sq3_buf[guide, row] = squares(own_float)
    sq_copies = []
    for k in range(n):
        targets = [{"row": peer("row", k), "guide": other}]
        if k:
            targets.append({"row": peer("row", k)})
        for number, target in zip((0, 1), targets):
            copy = pltpu.make_async_remote_copy(
                src_ref=sq3_buf.at[guide, row],
                dst_ref=sq3_buf.at[guide, row],
                send_sem=sq_sem.at[0, number, k],
                recv_sem=sq_sem.at[1, number, k],
                device_id=target,
                device_id_type=MESH,
            )
            copy.start()
            sq_copies.append(copy)
    next_input = (own_float * next_gain_ref[...].astype(F32)[None, :]).astype(BF16)
    loads[6].wait()
    np_buf[row, :, 0:width_q] = mm(next_input, wnq[...]).astype(BF16)
    loads[7].wait()
    pairs_to(np_buf, next_input, wnkv)
    finish(two_copies)
    first = guide == 0

    def my_half(values):
        return jnp.where(first, values[:half_rows], values[half_rows:])

    both = jnp.concatenate(
        [my_half(two_buf[0].astype(F32)), my_half(two_buf[1].astype(F32))], axis=0
    )
    np_copies = spread(np_buf, "row", 10)
    head_input = (both * final_gain_ref[...].astype(F32)[None, :]).astype(BF16)

    guidance_row = jnp.zeros((1, requests), F32)
    for k in range(TENANTS):
        guidance_row = guidance_row + jnp.where(tenant_ref[...] == k, guide_ref[k], 0.0)
    here = iota((half_rows, requests), 1) == iota((half_rows, requests), 0) + guide * half_rows
    guidance = jnp.sum(jnp.where(here, guidance_row, 0.0), axis=1, keepdims=True)

    def raw(rows):
        return lax.dot_general(
            head_input, rows, (((1,), (1,)), ((), ())), preferred_element_type=F32
        )

    vocab = wh.shape[0]
    window = window_of(share)
    half = window // 2
    chunk = 1024 if half % 1024 == 0 else half
    whole = vocab // LANES * LANES
    last_start = (n - 1) * share // LANES * LANES
    pieces = [(at, min(chunk, share - at)) for at in range(0, share, chunk)]
    copies = []
    head_loads[0].wait()
    if exact:
        part[...] = jnp.zeros(part.shape, F32)
        for at, size in pieces:
            start = pl.multiple_of(peer("row", 1) * share + at, SUBLANES)
            first_part[:, at : at + size] = raw(wh[pl.ds(start, size), :])

    finish(sq_copies)
    sums = [total(sq3_buf.at[side], n) for side in range(2)]
    own_scale = scale_of(jnp.where(first, sums[0], sums[1]))[:, 0:1]
    factor_c = guidance * scale_of(my_half(sums[0]))[:, 0:1]
    factor_u = (1.0 - guidance) * scale_of(my_half(sums[1]))[:, 0:1]

    def blend(logits):
        return factor_c * logits[:half_rows] + factor_u * logits[half_rows:]

    def guided(rows):
        return blend(raw(rows))

    if not exact:
        part[:, whole : part.shape[1]] = jnp.zeros((half_rows, part.shape[1] - whole), F32)
        if whole < vocab:
            part[:, whole:vocab] = guided(wh[whole:vocab, :])
    for k in range(1, n + 1):
        dest = peer("row", k)
        if exact:
            if k > 1:
                head_loads[k - 1].wait()
            for first_row, size in pieces:
                at = pl.multiple_of(dest * share + first_row, SUBLANES)
                top = first_row // half * half_rows
                column = first_row % half
                if k == 1:
                    value = blend(first_part[:, first_row : first_row + size])
                else:
                    value = guided(wh[pl.ds(at, size), :])
                part[top : top + half_rows, column : column + size] = value
            stacked = part[...]
        else:
            start = dest * share // LANES * LANES
            is_last = (dest + 1) // n
            for piece in range(window // chunk):
                over = max(0, last_start + (piece + 1) * chunk - whole)
                at = pl.multiple_of(start + piece * chunk - is_last * over, LANES)
                part[:, pl.ds(at, chunk)] = guided(wh[pl.ds(at, chunk), :])
            start = pl.multiple_of(start, LANES)
            upper = pl.multiple_of(start + half, LANES)
            stacked = jnp.concatenate(
                [part[:, pl.ds(start, half)], part[:, pl.ds(upper, half)]], axis=0
            )
        if k < n:
            h_send[k - 1] = stacked.astype(BF16)
            copies.append(send(h_send.at[k - 1], h_buf.at[row], "row", 11, k))
        else:
            h_buf[row] = stacked.astype(BF16)

    finish(np_copies)
    sums = own_scale * total(np_buf, n)
    nq_ref[...] = sums[:, :width_q].astype(BF16)
    nkv_ref[...] = sums[:, width_q:].astype(BF16)

    finish(copies)
    sums = total(h_buf, n)
    if exact:
        out_ref[:, 0:half] = sums[:half_rows]
        out_ref[:, half:share] = sums[half_rows:, 0 : share - half]
    else:
        part[:, 0:half] = sums[:half_rows]
        part[:, half:window] = sums[half_rows:]
        offset = lax.rem(row * share, LANES)
        turn = lax.rem(LANES - offset, LANES)
        lane8 = iota((half_rows, LANES), 1)
        for j in range(-(-share // LANES)):
            here_tile = pltpu.roll(part[:, j * LANES : (j + 1) * LANES], turn, 1)
            next_tile = pltpu.roll(part[:, (j + 1) * LANES : (j + 2) * LANES], turn, 1)
            joined = jnp.where(lane8 < LANES - offset, here_tile, next_tile)
            wide = min(LANES, share - j * LANES)
            out_ref[:, j * LANES : j * LANES + wide] = joined[:, :wide]
    for copy in pending:
        copy.wait_send()


def local(
    n,
    m,
    hidden,
    lengths,
    kv_cache,
    attn_gain,
    w_query,
    w_key_value,
    w_out,
    mlp_gain,
    w_gate_up,
    w_down,
    final_gain,
    w_head,
    next_gain,
    w_next_query,
    w_next_kv,
    tenant,
    guide_scale,
):
    x_rows = hidden[0]
    requests, width = x_rows.shape
    cache = kv_cache[0]
    head_rows = w_head.T
    weights = (cache, w_query, w_key_value, w_out, w_gate_up, w_down, head_rows, w_next_query, w_next_kv)
    width_q = w_query.shape[1]
    width_kv = 2 * w_key_value.shape[2]
    heads_here = width_q // HD
    hidden_here = w_down.shape[0]
    block = hidden_here // n
    vocab = head_rows.shape[0]
    share = vocab // n
    window = window_of(share)
    last_start = (n - 1) * share // LANES * LANES
    exact = share % SUBLANES == 0
    part_shape = (requests, window // 2) if exact else (requests // 2, last_start + window)
    first_shape = (requests, window) if exact else (requests, LANES)
    scattered = block % LANES == 0
    gu_width = 2 * block if scattered else 2 * hidden_here
    peers = max(n, m) - 1
    vmem = pl.BlockSpec(memory_space=pltpu.VMEM)
    smem = pl.BlockSpec(memory_space=pltpu.SMEM)
    hbm = pl.BlockSpec(memory_space=pl.ANY)
    scratch = [pltpu.VMEM(a.shape, a.dtype) for a in weights] + [
        pltpu.VMEM((width, 2 * width), BF16),
        pltpu.VMEM((n, requests, width_q + width_kv), BF16),
        pltpu.VMEM((n, requests, LANES), F32),
        pltpu.VMEM((requests, heads_here, LANES), F32),
        pltpu.VMEM((n, requests, LANES), F32),
        pltpu.VMEM((n, requests, width_q), BF16),
        pltpu.VMEM((m, requests, width), BF16),
        pltpu.VMEM((n, requests, LANES), F32),
        pltpu.VMEM((n - 1 if scattered else 1, requests, gu_width), BF16),
        pltpu.VMEM((n, requests, gu_width), BF16),
        pltpu.VMEM((n, requests, block), BF16),
        pltpu.VMEM((m, requests, width), BF16),
        pltpu.VMEM((2, requests, width), BF16),
        pltpu.VMEM((2, n, requests, LANES), F32),
        pltpu.VMEM((n, requests, width_q + width_kv), BF16),
        pltpu.VMEM(first_shape, F32),
        pltpu.VMEM(part_shape, F32),
        pltpu.VMEM((n - 1, requests, window // 2), BF16),
        pltpu.VMEM((n, requests, window // 2), BF16),
        pltpu.SemaphoreType.DMA((8 + n,)),
        pltpu.SemaphoreType.DMA((14, peers)),
        pltpu.SemaphoreType.DMA((14, peers)),
        pltpu.SemaphoreType.DMA((2, 2, n)),
    ]
    guided, next_query, next_pairs = pl.pallas_call(
        functools.partial(layer_kernel, n, m),
        out_shape=(
            jax.ShapeDtypeStruct((requests // 2, share), F32),
            jax.ShapeDtypeStruct((requests, width_q), BF16),
            jax.ShapeDtypeStruct((requests, width_kv), BF16),
        ),
        in_specs=[vmem, vmem, vmem, smem] + [vmem] * 4 + [hbm] * 9,
        out_specs=(vmem, vmem, vmem),
        scratch_shapes=scratch,
        compiler_params=pltpu.CompilerParams(
            collective_id=0, has_side_effects=True, vmem_limit_bytes=60 * 1024 * 1024
        ),
        name="decode_layer",
    )(x_rows, lengths, tenant.reshape(1, -1), guide_scale, attn_gain, mlp_gain, final_gain, next_gain, *weights)
    return (guided, next_query[None], next_pairs.reshape(1, requests, 2, -1))


def solution(mesh):
    placed = (
        P("guide", None, "row"),
        P("guide", None),
        P("guide", None, None, "row", "col"),
        P("row"),
        P("row", "col"),
        P("row", None, "col"),
        P("col", "row"),
        P("row"),
        P("row", None, "col"),
        P("col", "row"),
        P("row"),
        P("row", "col"),
        P("row"),
        P("row", "col"),
        P("row", None, "col"),
        P(),
        P(),
    )
    return jax.shard_map(
        functools.partial(local, mesh.shape["row"], mesh.shape["col"]),
        mesh=mesh,
        in_specs=placed,
        out_specs=(
            P("guide", ("col", "row")),
            P("guide", None, "col"),
            P("guide", None, None, "col"),
        ),
        check_vma=False,
    )
```

```python
import functools
import math

import jax
import jax.numpy as jnp
from jax import lax
from jax.experimental import pallas as pl
from jax.experimental.pallas import tpu as pltpu
from jax.sharding import PartitionSpec as P

D = 2048
HEADS = 32
KVH = 8
HD = 64
TENANTS = 4
EPSILON = 1e-05
ROPE_BASE = 500000.0
NEGATIVE = -1e30
LANES = 128
SUBLANES = 16
F32 = jnp.float32
BF16 = jnp.bfloat16
MESH = pl.DeviceIdType.MESH


def mm(a, b):
    return jnp.dot(a, b, preferred_element_type=F32)


def iota(shape, dim):
    return lax.broadcasted_iota(jnp.int32, shape, dim)


def window_of(block):
    tiles = -(-(block + LANES - 1) // LANES)
    return (tiles + tiles % 2) * LANES


def layer_kernel(
    n,
    m,
    x_ref,
    len_ref,
    tenant_ref,
    guide_ref,
    attn_gain_ref,
    mlp_gain_ref,
    final_gain_ref,
    next_gain_ref,
    kv_hbm,
    wq_hbm,
    wkv_hbm,
    wo_hbm,
    wgu_hbm,
    wd_hbm,
    wh_hbm,
    wnq_hbm,
    wnkv_hbm,
    out_ref,
    next_ref,
    kv,
    wq,
    wkv,
    wo,
    wgu,
    wd,
    wh,
    wnq,
    wnkv,
    weaver,
    flat,
    q_buf,
    sq_buf,
    q_rows,
    stat_buf,
    a_buf,
    o_buf,
    sq2_buf,
    gu_send,
    gu_buf,
    act_buf,
    d_buf,
    one_buf,
    sq3_buf,
    np_buf,
    first_part,
    part,
    h_send,
    h_buf,
    local_sem,
    send_sem,
    recv_sem,
    d_sem,
):
    row = lax.axis_index("row")
    col = lax.axis_index("col")
    guide = lax.axis_index("guide")
    place = {"row": (row, n), "col": (col, m), "guide": (guide, 2)}

    pairs = [
        (wq_hbm, wq),
        (wkv_hbm, wkv),
        (kv_hbm, kv),
        (wo_hbm, wo),
        (wgu_hbm, wgu),
        (wd_hbm, wd),
        (wnq_hbm, wnq),
        (wnkv_hbm, wnkv),
    ]
    loads = [pltpu.make_async_copy(a, b, local_sem.at[i]) for i, (a, b) in enumerate(pairs)]
    for load in loads:
        load.start()
    share = wh.shape[0] // n
    exact = share % SUBLANES == 0
    if exact:
        head_loads = []
        for k in range(1, n + 1):
            at = pl.ds(pl.multiple_of(lax.rem(row + k, n) * share, SUBLANES), share)
            head_loads.append(
                pltpu.make_async_copy(wh_hbm.at[at, :], wh.at[at, :], local_sem.at[7 + k])
            )
    else:
        head_loads = [pltpu.make_async_copy(wh_hbm, wh, local_sem.at[8])]
    early = (len(head_loads) + 1) // 2

    pending = []

    def peer(axis, k):
        me, size = place[axis]
        return lax.rem(me + k, size)

    other = 1 - guide
    barrier = pltpu.get_barrier_semaphore()
    for k in range(1, m):
        target = {"col": peer("col", k), "guide": other}
        pl.semaphore_signal(barrier, inc=1, device_id=target, device_id_type=MESH)
    for axis in ("row", "col", "guide"):
        for k in range(1, place[axis][1]):
            pl.semaphore_signal(barrier, inc=1, device_id={axis: peer(axis, k)}, device_id_type=MESH)

    def send(source, target, axis, number, k):
        copy = pltpu.make_async_remote_copy(
            src_ref=source,
            dst_ref=target,
            send_sem=send_sem.at[number, k - 1],
            recv_sem=recv_sem.at[number, k - 1],
            device_id={axis: peer(axis, k)},
            device_id_type=MESH,
        )
        copy.start()
        return copy

    def spread(buf, axis, number):
        me, size = place[axis]
        return [send(buf.at[me], buf.at[me], axis, number, k) for k in range(1, size)]

    def finish(copies):
        for copy in copies:
            copy.wait_recv()
            pending.append(copy)

    def total(buf, size):
        result = buf[0].astype(F32)
        for k in range(1, size):
            result = result + buf[k].astype(F32)
        return result

    def squares(values):
        return jnp.broadcast_to(jnp.sum(values * values, axis=1, keepdims=True), (values.shape[0], LANES))

    def scale_of(sums):
        return lax.rsqrt(sums / D + EPSILON)

    requests = x_ref.shape[0]
    depth = wgu.shape[0]
    width_q = wq.shape[1]
    key_width = wkv.shape[2]
    width_kv = 2 * key_width
    weaver[...] = (iota((depth, 2 * depth), 1) == 2 * iota((depth, 2 * depth), 0)).astype(BF16)

    def weave(values):
        even = mm(values, weaver[...])
        return jnp.concatenate([even, pltpu.roll(even, 1, 1)], axis=0).astype(BF16)

    def flatten(low_row, high_row):
        flat[2 * low_row : 2 * high_row, :] = wgu[low_row:high_row].reshape(
            2 * (high_row - low_row), wgu.shape[2]
        )

    def pairs_to(buf, values, weights):
        both_parts = mm(weave(values), weights[...].reshape(2 * depth, weights.shape[2]))
        buf[row, :, width_q : width_q + key_width] = both_parts[:requests].astype(BF16)
        buf[row, :, width_q + key_width : width_q + width_kv] = both_parts[requests:].astype(BF16)

    half_rows = requests // 2
    x_float = x_ref[...].astype(F32)
    normed = (x_float * attn_gain_ref[...].astype(F32)[None, :]).astype(BF16)
    sq_buf[row] = squares(x_float)
    loads[0].wait()
    q_buf[row, :, 0:width_q] = mm(normed, wq[...]).astype(BF16)
    loads[1].wait()
    pairs_to(q_buf, normed, wkv)
    pl.semaphore_wait(barrier, n - 1 + 2 * (m - 1) + 1)
    copies = spread(sq_buf, "row", 0) + spread(q_buf, "row", 1)
    for load in head_loads[:early]:
        load.start()

    lane = iota((requests, LANES), 1)
    lengths_row = len_ref[...].astype(F32)
    pick = iota((requests, requests), 0) == iota((requests, requests), 1)
    length_col = jnp.sum(jnp.where(pick, lengths_row, 0.0), axis=1, keepdims=True)
    frequency = jnp.exp((lane % (HD // 2)).astype(F32) * (-2.0 * math.log(ROPE_BASE) / HD))
    angles = length_col * frequency
    cosine = jnp.cos(angles)
    sine = jnp.sin(angles)
    low = (lane % HD) < HD // 2
    signed = jnp.where(low, -sine, sine)
    left = lane < HD

    def rotated(tile):
        ahead = pltpu.roll(tile, LANES - HD // 2, 1)
        behind = pltpu.roll(tile, HD // 2, 1)
        return tile * cosine + jnp.where(low, ahead, behind) * signed

    finish(copies)
    scale = scale_of(total(sq_buf, n))
    sums = total(q_buf, n)
    tiles = [scale * sums[:, t * LANES : (t + 1) * LANES] for t in range((width_q + width_kv) // LANES)]
    q_tiles = width_q // LANES
    heads_here = 2 * q_tiles
    group = HEADS // KVH
    for t in range(q_tiles):
        tile = rotated(tiles[t]).astype(BF16).astype(F32)
        swapped = pltpu.roll(tile, HD, 1)
        for side in range(2):
            j = 2 * t + side
            kv_head = j // group
            wanted = tile if side == kv_head else swapped
            q_rows[:, j, :] = jnp.where(left == (kv_head == 0), wanted, 0.0)
    new_key = rotated(tiles[q_tiles]).astype(BF16).astype(F32)
    new_value = tiles[q_tiles + 1].astype(BF16).astype(F32)

    loads[2].wait()
    inv_scale = HD**-0.5
    span = kv.shape[2]
    rows3 = (requests, heads_here, LANES)
    q3 = q_rows[...]
    scores = jnp.stack(
        [
            lax.dot_general(
                q3[b].astype(BF16), kv[b, 0], (((1,), (1,)), ((), ())), preferred_element_type=F32
            )
            for b in range(requests)
        ]
    ) * inv_scale
    own_score = jnp.sum(q3 * new_key[:, None, :], axis=2, keepdims=True) * inv_scale
    length3 = length_col[:, :, None]
    position = (row * span + iota((requests, heads_here, span), 2)).astype(F32)
    usable = position < length3
    masked = jnp.where(usable, scores, NEGATIVE)
    best = jnp.max(masked, axis=2, keepdims=True)
    terms = jnp.where(usable, jnp.exp(masked - best), 0.0)
    norm = jnp.sum(terms, axis=2, keepdims=True)
    weighted = jnp.stack([mm(terms[b].astype(BF16), kv[b, 1]) for b in range(requests)])
    lane3 = iota(rows3, 2)
    q_rows[...] = weighted

    def to_lanes(column):
        return jnp.sum(jnp.where(lane3 == iota(rows3, 1), column, 0.0), axis=1)

    def by_head(table, t):
        return jnp.where(left, table[:, 2 * t : 2 * t + 1], table[:, 2 * t + 1 : 2 * t + 2])

    stat_buf[row] = jnp.where(left, to_lanes(best), pltpu.roll(to_lanes(norm), HD, 1))
    for t in range(q_tiles):
        even = q_rows[:, 2 * t, :]
        odd = q_rows[:, 2 * t + 1, :]
        if 2 * t < group:
            tile = jnp.where(left, even, pltpu.roll(odd, HD, 1))
        else:
            tile = jnp.where(left, pltpu.roll(even, HD, 1), odd)
        a_buf[row, :, t * LANES : (t + 1) * LANES] = tile.astype(BF16)
    copies = spread(stat_buf, "row", 12) + spread(a_buf, "row", 2)
    for load in head_loads[early:]:
        load.start()
    own_lanes = to_lanes(own_score)
    loads[4].wait()
    hidden_here = wgu.shape[2]
    flatten(0, depth // 2)
    turned_value = pltpu.roll(new_value, HD, 1)
    value_of = (jnp.where(left, new_value, turned_value), jnp.where(left, turned_value, new_value))
    finish(copies)
    bests = [stat_buf[k] for k in range(n)]
    final_best = own_lanes
    for value in bests:
        final_best = jnp.maximum(final_best, value)
    own_exp = jnp.exp(own_lanes - final_best)
    factors = [jnp.exp(value - final_best) for value in bests]
    norm_sum = own_exp
    for k in range(n):
        norm_sum = norm_sum + pltpu.roll(bests[k], HD, 1) * factors[k]
    own_factor = own_exp.astype(BF16).astype(F32)
    att_tiles = []
    for t in range(q_tiles):
        tile = by_head(own_factor, t) * value_of[2 * t // group]
        for k in range(n):
            tile = tile + by_head(factors[k], t) * a_buf[k, :, t * LANES : (t + 1) * LANES].astype(F32)
        att_tiles.append(tile / by_head(norm_sum, t))
    attended2 = jnp.concatenate(att_tiles, axis=1).astype(BF16)

    loads[3].wait()
    o_buf[col] = mm(attended2, wo[...]).astype(BF16)
    copies = spread(o_buf, "col", 3)
    flatten(depth // 2, depth)
    finish(copies)
    one_float = (x_float + total(o_buf, m)).astype(BF16).astype(F32)

    one_buf[guide] = one_float.astype(BF16)
    one_copies = spread(one_buf, "guide", 8)

    sq2_buf[row] = squares(one_float)
    sq_copies = spread(sq2_buf, "row", 4)
    mlp_input = (one_float * mlp_gain_ref[...].astype(F32)[None, :]).astype(BF16)
    block = hidden_here // n
    woven = weave(mlp_input)
    if block % LANES == 0:
        copies = []
        for k in range(1, n + 1):
            dest = peer("row", k)
            start = pl.multiple_of(dest * block, LANES)
            both_parts = mm(woven, flat[:, pl.ds(start, block)])
            joined = jnp.concatenate([both_parts[:requests], both_parts[requests:]], axis=1).astype(BF16)
            if k < n:
                gu_send[k - 1] = joined
                copies.append(send(gu_send.at[k - 1], gu_buf.at[row], "row", 5, k))
            else:
                gu_buf[row] = joined
        finish(sq_copies)
        mlp_scale = scale_of(total(sq2_buf, n))[:, 0:1]
        finish(copies)
        sums = total(gu_buf, n) * mlp_scale
        gate, up = sums[:, :block], sums[:, block:]
        act_buf[row] = (gate / (1.0 + jnp.exp(-gate)) * up).astype(BF16)
        copies = spread(act_buf, "row", 6)
        loads[5].wait()
        down = mm(act_buf[row], wd[pl.ds(pl.multiple_of(row * block, LANES), block), :])
        for k in range(1, n):
            finish(copies[k - 1 : k])
            source = lax.rem(row - k + n, n)
            start = pl.multiple_of(source * block, LANES)
            down = down + mm(act_buf[source], wd[pl.ds(start, block), :])
    else:
        both_parts = mm(woven, flat[...])
        gu_buf[row, :, 0:hidden_here] = both_parts[:requests].astype(BF16)
        gu_buf[row, :, hidden_here : 2 * hidden_here] = both_parts[requests:].astype(BF16)
        copies = spread(gu_buf, "row", 5)
        finish(sq_copies)
        mlp_scale = scale_of(total(sq2_buf, n))[:, 0:1]
        finish(copies)
        sums = total(gu_buf, n) * mlp_scale
        gate, up = sums[:, :hidden_here], sums[:, hidden_here:]
        loads[5].wait()
        down = mm((gate / (1.0 + jnp.exp(-gate)) * up).astype(BF16), wd[...])
    d_buf[guide, col] = down.astype(BF16)
    d_copies = []
    for k in range(m):
        targets = [{"col": peer("col", k), "guide": other}]
        if k:
            targets.append({"col": peer("col", k)})
        for number, target in zip((0, 1), targets):
            copy = pltpu.make_async_remote_copy(
                src_ref=d_buf.at[guide, col],
                dst_ref=d_buf.at[guide, col],
                send_sem=d_sem.at[0, number, k],
                recv_sem=d_sem.at[1, number, k],
                device_id=target,
                device_id_type=MESH,
            )
            copy.start()
            d_copies.append(copy)
    finish(one_copies)
    finish(d_copies)

    twos = [
        (one_buf[side].astype(F32) + total(d_buf.at[side], m)).astype(BF16).astype(F32)
        for side in range(2)
    ]
    sq3_buf[row] = jnp.where(left, squares(twos[0]), squares(twos[1]))
    sq_copies = spread(sq3_buf, "row", 9)
    first = guide == 0
    own_float = jnp.where(first, twos[0], twos[1])
    next_input = (own_float * next_gain_ref[...].astype(F32)[None, :]).astype(BF16)
    loads[6].wait()
    np_buf[row, :, 0:width_q] = mm(next_input, wnq[...]).astype(BF16)
    loads[7].wait()
    pairs_to(np_buf, next_input, wnkv)

    def my_half(values):
        return jnp.where(first, values[:half_rows], values[half_rows:])

    both = jnp.concatenate(
        [my_half(twos[0]), my_half(twos[1])], axis=0
    )
    np_copies = spread(np_buf, "row", 10)
    head_input = (both * final_gain_ref[...].astype(F32)[None, :]).astype(BF16)

    guidance_row = jnp.zeros((1, requests), F32)
    for k in range(TENANTS):
        guidance_row = guidance_row + jnp.where(tenant_ref[...] == k, guide_ref[k], 0.0)
    here = iota((half_rows, requests), 1) == iota((half_rows, requests), 0) + guide * half_rows
    guidance = jnp.sum(jnp.where(here, guidance_row, 0.0), axis=1, keepdims=True)

    def raw(rows):
        return lax.dot_general(
            head_input, rows, (((1,), (1,)), ((), ())), preferred_element_type=F32
        )

    vocab = wh.shape[0]
    window = window_of(share)
    half = window // 2
    chunk = 1024 if half % 1024 == 0 else half
    whole = vocab // LANES * LANES
    last_start = (n - 1) * share // LANES * LANES
    pieces = [(at, min(chunk, share - at)) for at in range(0, share, chunk)]
    copies = []
    head_loads[0].wait()
    if exact:
        part[...] = jnp.zeros(part.shape, F32)
        for at, size in pieces:
            start = pl.multiple_of(peer("row", 1) * share + at, SUBLANES)
            first_part[:, at : at + size] = raw(wh[pl.ds(start, size), :])

    finish(sq_copies)
    scales = scale_of(total(sq3_buf, n))
    sides = [scales[:, 0:1], scales[:, HD : HD + 1]]
    own_scale = jnp.where(first, sides[0], sides[1])
    factor_c = guidance * my_half(sides[0])
    factor_u = (1.0 - guidance) * my_half(sides[1])

    def blend(logits):
        return factor_c * logits[:half_rows] + factor_u * logits[half_rows:]

    def guided(rows):
        return blend(raw(rows))

    if not exact:
        part[:, whole : part.shape[1]] = jnp.zeros((half_rows, part.shape[1] - whole), F32)
        if whole < vocab:
            part[:, whole:vocab] = guided(wh[whole:vocab, :])
    for k in range(1, n + 1):
        dest = peer("row", k)
        if exact:
            if k > 1:
                head_loads[k - 1].wait()
            for first_row, size in pieces:
                at = pl.multiple_of(dest * share + first_row, SUBLANES)
                top = first_row // half * half_rows
                column = first_row % half
                if k == 1:
                    value = blend(first_part[:, first_row : first_row + size])
                else:
                    value = guided(wh[pl.ds(at, size), :])
                part[top : top + half_rows, column : column + size] = value
            stacked = part[...]
        else:
            start = dest * share // LANES * LANES
            is_last = (dest + 1) // n
            for piece in range(window // chunk):
                over = max(0, last_start + (piece + 1) * chunk - whole)
                at = pl.multiple_of(start + piece * chunk - is_last * over, LANES)
                part[:, pl.ds(at, chunk)] = guided(wh[pl.ds(at, chunk), :])
            start = pl.multiple_of(start, LANES)
            upper = pl.multiple_of(start + half, LANES)
            stacked = jnp.concatenate(
                [part[:, pl.ds(start, half)], part[:, pl.ds(upper, half)]], axis=0
            )
        if k < n:
            h_send[k - 1] = stacked.astype(BF16)
            copies.append(send(h_send.at[k - 1], h_buf.at[row], "row", 11, k))
        else:
            h_buf[row] = stacked.astype(BF16)

    finish(np_copies)
    sums = own_scale * total(np_buf, n)
    next_ref[...] = sums.astype(BF16)

    finish(copies)
    sums = total(h_buf, n)
    if exact:
        out_ref[:, 0:half] = sums[:half_rows]
        out_ref[:, half:share] = sums[half_rows:, 0 : share - half]
    else:
        part[:, 0:half] = sums[:half_rows]
        part[:, half:window] = sums[half_rows:]
        offset = lax.rem(row * share, LANES)
        turn = lax.rem(LANES - offset, LANES)
        lane8 = iota((half_rows, LANES), 1)
        for j in range(-(-share // LANES)):
            here_tile = pltpu.roll(part[:, j * LANES : (j + 1) * LANES], turn, 1)
            next_tile = pltpu.roll(part[:, (j + 1) * LANES : (j + 2) * LANES], turn, 1)
            joined = jnp.where(lane8 < LANES - offset, here_tile, next_tile)
            wide = min(LANES, share - j * LANES)
            out_ref[:, j * LANES : j * LANES + wide] = joined[:, :wide]
    for copy in pending:
        copy.wait_send()


def part_outputs(guided_ref, next_ref, out_ref, query_ref, pairs_ref):
    out_ref[...] = guided_ref[...]
    width_q = query_ref.shape[1]
    width = pairs_ref.shape[2]
    query_ref[...] = next_ref[:, 0:width_q]
    for k in range(2):
        pairs_ref[:, k, :] = next_ref[:, width_q + k * width : width_q + (k + 1) * width]


def local(
    n,
    m,
    hidden,
    lengths,
    kv_cache,
    attn_gain,
    w_query,
    w_key_value,
    w_out,
    mlp_gain,
    w_gate_up,
    w_down,
    final_gain,
    w_head,
    next_gain,
    w_next_query,
    w_next_kv,
    tenant,
    guide_scale,
):
    x_rows = hidden[0]
    requests, width = x_rows.shape
    cache = kv_cache[0]
    head_rows = w_head.T
    weights = (cache, w_query, w_key_value, w_out, w_gate_up, w_down, head_rows, w_next_query, w_next_kv)
    width_q = w_query.shape[1]
    width_kv = 2 * w_key_value.shape[2]
    heads_here = width_q // HD
    hidden_here = w_down.shape[0]
    block = hidden_here // n
    vocab = head_rows.shape[0]
    share = vocab // n
    window = window_of(share)
    last_start = (n - 1) * share // LANES * LANES
    exact = share % SUBLANES == 0
    part_shape = (requests, window // 2) if exact else (requests // 2, last_start + window)
    first_shape = (requests, window) if exact else (requests, LANES)
    scattered = block % LANES == 0
    gu_width = 2 * block if scattered else 2 * hidden_here
    peers = max(n, m) - 1
    vmem = pl.BlockSpec(memory_space=pltpu.VMEM)
    smem = pl.BlockSpec(memory_space=pltpu.SMEM)
    hbm = pl.BlockSpec(memory_space=pl.ANY)
    scratch = [pltpu.VMEM(a.shape, a.dtype) for a in weights] + [
        pltpu.VMEM((width, 2 * width), BF16),
        pltpu.VMEM((2 * width, hidden_here), BF16),
        pltpu.VMEM((n, requests, width_q + width_kv), BF16),
        pltpu.VMEM((n, requests, LANES), F32),
        pltpu.VMEM((requests, heads_here, LANES), F32),
        pltpu.VMEM((n, requests, LANES), F32),
        pltpu.VMEM((n, requests, width_q), BF16),
        pltpu.VMEM((m, requests, width), BF16),
        pltpu.VMEM((n, requests, LANES), F32),
        pltpu.VMEM((n - 1 if scattered else 1, requests, gu_width), BF16),
        pltpu.VMEM((n, requests, gu_width), BF16),
        pltpu.VMEM((n, requests, block), BF16),
        pltpu.VMEM((2, m, requests, width), BF16),
        pltpu.VMEM((2, requests, width), BF16),
        pltpu.VMEM((n, requests, LANES), F32),
        pltpu.VMEM((n, requests, width_q + width_kv), BF16),
        pltpu.VMEM(first_shape, F32),
        pltpu.VMEM(part_shape, F32),
        pltpu.VMEM((n - 1, requests, window // 2), BF16),
        pltpu.VMEM((n, requests, window // 2), BF16),
        pltpu.SemaphoreType.DMA((8 + n,)),
        pltpu.SemaphoreType.DMA((14, peers)),
        pltpu.SemaphoreType.DMA((14, peers)),
        pltpu.SemaphoreType.DMA((2, 2, m)),
    ]
    guided, next_all = pl.pallas_call(
        functools.partial(layer_kernel, n, m),
        out_shape=(
            jax.ShapeDtypeStruct((requests // 2, share), F32),
            jax.ShapeDtypeStruct((requests, width_q + width_kv), BF16),
        ),
        in_specs=[vmem, vmem, vmem, smem] + [vmem] * 4 + [hbm] * 9,
        out_specs=(vmem, vmem),
        scratch_shapes=scratch,
        compiler_params=pltpu.CompilerParams(
            collective_id=0, has_side_effects=True, vmem_limit_bytes=60 * 1024 * 1024
        ),
        name="decode_layer",
    )(x_rows, lengths, tenant.reshape(1, -1), guide_scale, attn_gain, mlp_gain, final_gain, next_gain, *weights)
    guided, next_query, next_pairs = pl.pallas_call(
        part_outputs,
        out_shape=(
            jax.ShapeDtypeStruct(guided.shape, F32),
            jax.ShapeDtypeStruct((requests, width_q), BF16),
            jax.ShapeDtypeStruct((requests, 2, width_kv // 2), BF16),
        ),
        in_specs=[vmem, vmem],
        out_specs=(vmem, vmem, vmem),
        name="part_outputs",
    )(guided, next_all)
    return (guided, next_query[None], next_pairs[None])


def solution(mesh):
    placed = (
        P("guide", None, "row"),
        P("guide", None),
        P("guide", None, None, "row", "col"),
        P("row"),
        P("row", "col"),
        P("row", None, "col"),
        P("col", "row"),
        P("row"),
        P("row", None, "col"),
        P("col", "row"),
        P("row"),
        P("row", "col"),
        P("row"),
        P("row", "col"),
        P("row", None, "col"),
        P(),
        P(),
    )
    return jax.shard_map(
        functools.partial(local, mesh.shape["row"], mesh.shape["col"]),
        mesh=mesh,
        in_specs=placed,
        out_specs=(
            P("guide", ("col", "row")),
            P("guide", None, "col"),
            P("guide", None, None, "col"),
        ),
        check_vma=False,
    )
```

```python
import functools
import math

import jax
import jax.numpy as jnp
from jax import lax
from jax.experimental import pallas as pl
from jax.experimental.pallas import tpu as pltpu
from jax.sharding import PartitionSpec as P

D = 2048
HEADS = 32
KVH = 8
HD = 64
TENANTS = 4
EPSILON = 1e-05
ROPE_BASE = 500000.0
NEGATIVE = -1e30
LANES = 128
SUBLANES = 16
F32 = jnp.float32
BF16 = jnp.bfloat16
MESH = pl.DeviceIdType.MESH


def mm(a, b):
    return jnp.dot(a, b, preferred_element_type=F32)


def iota(shape, dim):
    return lax.broadcasted_iota(jnp.int32, shape, dim)


def window_of(block):
    tiles = -(-(block + LANES - 1) // LANES)
    return (tiles + tiles % 2) * LANES


def layer_kernel(
    n,
    m,
    x_ref,
    len_ref,
    tenant_ref,
    guide_ref,
    attn_gain_ref,
    mlp_gain_ref,
    final_gain_ref,
    next_gain_ref,
    kv_hbm,
    wq_hbm,
    wkv_hbm,
    wo_hbm,
    wgu_hbm,
    wd_hbm,
    wh_hbm,
    wnq_hbm,
    wnkv_hbm,
    out_ref,
    next_ref,
    kv,
    wq,
    wkv,
    wo,
    wgu,
    wd,
    wh,
    wnq,
    wnkv,
    weaver,
    flat,
    q_buf,
    sq_buf,
    q_rows,
    stat_buf,
    a_buf,
    o_buf,
    sq2_buf,
    gu_send,
    gu_buf,
    act_buf,
    d_buf,
    one_buf,
    sq3_buf,
    np_buf,
    first_part,
    part,
    h_send,
    h_buf,
    local_sem,
    send_sem,
    recv_sem,
    d_sem,
    h_sem,
):
    row = lax.axis_index("row")
    col = lax.axis_index("col")
    guide = lax.axis_index("guide")
    place = {"row": (row, n), "col": (col, m), "guide": (guide, 2)}

    pairs = [
        (wq_hbm, wq),
        (wkv_hbm, wkv),
        (kv_hbm, kv),
        (wo_hbm, wo),
        (wgu_hbm, wgu),
        (wd_hbm, wd),
        (wnq_hbm, wnq),
        (wnkv_hbm, wnkv),
    ]
    loads = [pltpu.make_async_copy(a, b, local_sem.at[i]) for i, (a, b) in enumerate(pairs)]
    for load in loads:
        load.start()
    share = wh_hbm.shape[0] // n
    exact = share % SUBLANES == 0 and window_of(share) % (8 * LANES) == 0
    if exact:
        head_loads = []
        for k in range(1, n + 1):
            at = pl.ds(pl.multiple_of(lax.rem(row + k, n) * share, SUBLANES), share)
            head_loads.append(
                pltpu.make_async_copy(wh_hbm.at[at, :], wh.at[at, :], local_sem.at[7 + k])
            )
    else:
        head_loads = [pltpu.make_async_copy(wh_hbm, wh, local_sem.at[8])]
    early = (len(head_loads) + 1) // 2

    pending = []

    def peer(axis, k):
        me, size = place[axis]
        return lax.rem(me + k, size)

    other = 1 - guide
    barrier = pltpu.get_barrier_semaphore()
    for k in range(1, m):
        target = {"col": peer("col", k), "guide": other}
        pl.semaphore_signal(barrier, inc=1, device_id=target, device_id_type=MESH)
    for axis in ("row", "col", "guide"):
        for k in range(1, place[axis][1]):
            pl.semaphore_signal(barrier, inc=1, device_id={axis: peer(axis, k)}, device_id_type=MESH)

    def send(source, target, axis, number, k):
        copy = pltpu.make_async_remote_copy(
            src_ref=source,
            dst_ref=target,
            send_sem=send_sem.at[number, k - 1],
            recv_sem=recv_sem.at[number, k - 1],
            device_id={axis: peer(axis, k)},
            device_id_type=MESH,
        )
        copy.start()
        return copy

    def spread(buf, axis, number):
        me, size = place[axis]
        return [send(buf.at[me], buf.at[me], axis, number, k) for k in range(1, size)]

    def finish(copies):
        for copy in copies:
            copy.wait_recv()
            pending.append(copy)

    def total(buf, size):
        result = buf[0].astype(F32)
        for k in range(1, size):
            result = result + buf[k].astype(F32)
        return result

    def squares(values):
        return jnp.broadcast_to(jnp.sum(values * values, axis=1, keepdims=True), (values.shape[0], LANES))

    def scale_of(sums):
        return lax.rsqrt(sums / D + EPSILON)

    requests = x_ref.shape[0]
    depth = wgu.shape[0]
    width_q = wq.shape[1]
    key_width = wkv.shape[2]
    width_kv = 2 * key_width
    weaver[...] = (iota((depth, 2 * depth), 1) == 2 * iota((depth, 2 * depth), 0)).astype(BF16)

    def weave(values):
        even = mm(values, weaver[...])
        return jnp.concatenate([even, pltpu.roll(even, 1, 1)], axis=0).astype(BF16)

    def flatten(low_row, high_row):
        flat[2 * low_row : 2 * high_row, :] = wgu[low_row:high_row].reshape(
            2 * (high_row - low_row), wgu.shape[2]
        )

    def pairs_to(buf, values, weights):
        both_parts = mm(weave(values), weights[...].reshape(2 * depth, weights.shape[2]))
        buf[row, :, width_q : width_q + key_width] = both_parts[:requests].astype(BF16)
        buf[row, :, width_q + key_width : width_q + width_kv] = both_parts[requests:].astype(BF16)

    half_rows = requests // 2
    x_float = x_ref[...].astype(F32)
    normed = (x_float * attn_gain_ref[...].astype(F32)[None, :]).astype(BF16)
    sq_buf[row] = squares(x_float)
    loads[0].wait()
    q_buf[row, :, 0:width_q] = mm(normed, wq[...]).astype(BF16)
    loads[1].wait()
    pairs_to(q_buf, normed, wkv)
    pl.semaphore_wait(barrier, n - 1 + 2 * (m - 1) + 1)
    copies = spread(sq_buf, "row", 0) + spread(q_buf, "row", 1)
    for load in head_loads[:early]:
        load.start()

    lane = iota((requests, LANES), 1)
    lengths_row = len_ref[...].astype(F32)
    pick = iota((requests, requests), 0) == iota((requests, requests), 1)
    length_col = jnp.sum(jnp.where(pick, lengths_row, 0.0), axis=1, keepdims=True)
    frequency = jnp.exp((lane % (HD // 2)).astype(F32) * (-2.0 * math.log(ROPE_BASE) / HD))
    angles = length_col * frequency
    cosine = jnp.cos(angles)
    sine = jnp.sin(angles)
    low = (lane % HD) < HD // 2
    signed = jnp.where(low, -sine, sine)
    left = lane < HD

    def rotated(tile):
        ahead = pltpu.roll(tile, LANES - HD // 2, 1)
        behind = pltpu.roll(tile, HD // 2, 1)
        return tile * cosine + jnp.where(low, ahead, behind) * signed

    finish(copies)
    scale = scale_of(total(sq_buf, n))
    sums = total(q_buf, n)
    tiles = [scale * sums[:, t * LANES : (t + 1) * LANES] for t in range((width_q + width_kv) // LANES)]
    q_tiles = width_q // LANES
    heads_here = 2 * q_tiles
    group = HEADS // KVH
    for t in range(q_tiles):
        tile = rotated(tiles[t]).astype(BF16).astype(F32)
        swapped = pltpu.roll(tile, HD, 1)
        for side in range(2):
            j = 2 * t + side
            kv_head = j // group
            wanted = tile if side == kv_head else swapped
            q_rows[:, j, :] = jnp.where(left == (kv_head == 0), wanted, 0.0)
    new_key = rotated(tiles[q_tiles]).astype(BF16).astype(F32)
    new_value = tiles[q_tiles + 1].astype(BF16).astype(F32)

    loads[2].wait()
    inv_scale = HD**-0.5
    span = kv.shape[2]
    rows3 = (requests, heads_here, LANES)
    q3 = q_rows[...]
    scores = jnp.stack(
        [
            lax.dot_general(
                q3[b].astype(BF16), kv[b, 0], (((1,), (1,)), ((), ())), preferred_element_type=F32
            )
            for b in range(requests)
        ]
    ) * inv_scale
    own_score = jnp.sum(q3 * new_key[:, None, :], axis=2, keepdims=True) * inv_scale
    length3 = length_col[:, :, None]
    position = (row * span + iota((requests, heads_here, span), 2)).astype(F32)
    usable = position < length3
    masked = jnp.where(usable, scores, NEGATIVE)
    best = jnp.max(masked, axis=2, keepdims=True)
    terms = jnp.where(usable, jnp.exp(masked - best), 0.0)
    norm = jnp.sum(terms, axis=2, keepdims=True)
    weighted = jnp.stack([mm(terms[b].astype(BF16), kv[b, 1]) for b in range(requests)])
    lane3 = iota(rows3, 2)
    q_rows[...] = weighted

    def to_lanes(column):
        return jnp.sum(jnp.where(lane3 == iota(rows3, 1), column, 0.0), axis=1)

    def by_head(table, t):
        return jnp.where(left, table[:, 2 * t : 2 * t + 1], table[:, 2 * t + 1 : 2 * t + 2])

    stat_buf[row] = jnp.where(left, to_lanes(best), pltpu.roll(to_lanes(norm), HD, 1))
    for t in range(q_tiles):
        even = q_rows[:, 2 * t, :]
        odd = q_rows[:, 2 * t + 1, :]
        if 2 * t < group:
            tile = jnp.where(left, even, pltpu.roll(odd, HD, 1))
        else:
            tile = jnp.where(left, pltpu.roll(even, HD, 1), odd)
        a_buf[row, :, t * LANES : (t + 1) * LANES] = tile.astype(BF16)
    copies = spread(stat_buf, "row", 12) + spread(a_buf, "row", 2)
    for load in head_loads[early:]:
        load.start()
    own_lanes = to_lanes(own_score)
    loads[4].wait()
    hidden_here = wgu.shape[2]
    flatten(0, depth // 2)
    turned_value = pltpu.roll(new_value, HD, 1)
    value_of = (jnp.where(left, new_value, turned_value), jnp.where(left, turned_value, new_value))
    finish(copies)
    bests = [stat_buf[k] for k in range(n)]
    final_best = own_lanes
    for value in bests:
        final_best = jnp.maximum(final_best, value)
    own_exp = jnp.exp(own_lanes - final_best)
    factors = [jnp.exp(value - final_best) for value in bests]
    norm_sum = own_exp
    for k in range(n):
        norm_sum = norm_sum + pltpu.roll(bests[k], HD, 1) * factors[k]
    own_factor = own_exp.astype(BF16).astype(F32)
    att_tiles = []
    for t in range(q_tiles):
        tile = by_head(own_factor, t) * value_of[2 * t // group]
        for k in range(n):
            tile = tile + by_head(factors[k], t) * a_buf[k, :, t * LANES : (t + 1) * LANES].astype(F32)
        att_tiles.append(tile / by_head(norm_sum, t))
    attended2 = jnp.concatenate(att_tiles, axis=1).astype(BF16)

    loads[3].wait()
    o_buf[col] = mm(attended2, wo[...]).astype(BF16)
    copies = spread(o_buf, "col", 3)
    flatten(depth // 2, depth)
    finish(copies)
    one_float = (x_float + total(o_buf, m)).astype(BF16).astype(F32)

    one_buf[guide] = one_float.astype(BF16)
    one_copies = spread(one_buf, "guide", 8)

    sq2_buf[row] = squares(one_float)
    sq_copies = spread(sq2_buf, "row", 4)
    mlp_input = (one_float * mlp_gain_ref[...].astype(F32)[None, :]).astype(BF16)
    block = hidden_here // n
    woven = weave(mlp_input)
    if block % LANES == 0:
        copies = []
        for k in range(1, n + 1):
            dest = peer("row", k)
            start = pl.multiple_of(dest * block, LANES)
            both_parts = mm(woven, flat[:, pl.ds(start, block)])
            joined = jnp.concatenate([both_parts[:requests], both_parts[requests:]], axis=1).astype(BF16)
            if k < n:
                gu_send[k - 1] = joined
                copies.append(send(gu_send.at[k - 1], gu_buf.at[row], "row", 5, k))
            else:
                gu_buf[row] = joined
        finish(sq_copies)
        mlp_scale = scale_of(total(sq2_buf, n))[:, 0:1]
        finish(copies)
        sums = total(gu_buf, n) * mlp_scale
        gate, up = sums[:, :block], sums[:, block:]
        act_buf[row] = (gate / (1.0 + jnp.exp(-gate)) * up).astype(BF16)
        copies = spread(act_buf, "row", 6)
        loads[5].wait()
        down = mm(act_buf[row], wd[pl.ds(pl.multiple_of(row * block, LANES), block), :])
        for k in range(1, n):
            finish(copies[k - 1 : k])
            source = lax.rem(row - k + n, n)
            start = pl.multiple_of(source * block, LANES)
            down = down + mm(act_buf[source], wd[pl.ds(start, block), :])
    else:
        both_parts = mm(woven, flat[...])
        gu_buf[row, :, 0:hidden_here] = both_parts[:requests].astype(BF16)
        gu_buf[row, :, hidden_here : 2 * hidden_here] = both_parts[requests:].astype(BF16)
        copies = spread(gu_buf, "row", 5)
        finish(sq_copies)
        mlp_scale = scale_of(total(sq2_buf, n))[:, 0:1]
        finish(copies)
        sums = total(gu_buf, n) * mlp_scale
        gate, up = sums[:, :hidden_here], sums[:, hidden_here:]
        loads[5].wait()
        down = mm((gate / (1.0 + jnp.exp(-gate)) * up).astype(BF16), wd[...])
    d_buf[guide, col] = down.astype(BF16)
    d_copies = []
    for k in range(m):
        targets = [{"col": peer("col", k), "guide": other}]
        if k:
            targets.append({"col": peer("col", k)})
        for number, target in zip((0, 1), targets):
            copy = pltpu.make_async_remote_copy(
                src_ref=d_buf.at[guide, col],
                dst_ref=d_buf.at[guide, col],
                send_sem=d_sem.at[0, number, k],
                recv_sem=d_sem.at[1, number, k],
                device_id=target,
                device_id_type=MESH,
            )
            copy.start()
            d_copies.append(copy)
    finish(one_copies)
    finish(d_copies)

    twos = [
        (one_buf[side].astype(F32) + total(d_buf.at[side], m)).astype(BF16).astype(F32)
        for side in range(2)
    ]
    sq3_buf[row] = jnp.where(left, squares(twos[0]), squares(twos[1]))
    sq_copies = spread(sq3_buf, "row", 9)
    first = guide == 0
    own_float = jnp.where(first, twos[0], twos[1])
    next_input = (own_float * next_gain_ref[...].astype(F32)[None, :]).astype(BF16)
    loads[6].wait()
    np_buf[row, :, 0:width_q] = mm(next_input, wnq[...]).astype(BF16)
    loads[7].wait()
    pairs_to(np_buf, next_input, wnkv)

    def my_half(values):
        return jnp.where(first, values[:half_rows], values[half_rows:])

    both = jnp.concatenate(
        [my_half(twos[0]), my_half(twos[1])], axis=0
    )
    np_copies = spread(np_buf, "row", 10)
    head_input = (both * final_gain_ref[...].astype(F32)[None, :]).astype(BF16)

    guidance_row = jnp.zeros((1, requests), F32)
    for k in range(TENANTS):
        guidance_row = guidance_row + jnp.where(tenant_ref[...] == k, guide_ref[k], 0.0)
    here = iota((half_rows, requests), 1) == iota((half_rows, requests), 0) + guide * half_rows
    guidance = jnp.sum(jnp.where(here, guidance_row, 0.0), axis=1, keepdims=True)

    def raw(rows):
        return lax.dot_general(
            head_input, rows, (((1,), (1,)), ((), ())), preferred_element_type=F32
        )

    vocab = share * n
    window = window_of(share)
    half = window // 2
    chunk = window // 8 if exact else half
    whole = vocab // LANES * LANES
    last_start = (n - 1) * share // LANES * LANES
    copies = []
    for load in head_loads:
        load.wait()
    sub = 4 * chunk

    def unit_rows(k, side, piece):
        at = peer("row", k) * share + side * sub + piece * chunk
        return wh[pl.ds(pl.multiple_of(at, SUBLANES), chunk), :]

    def fold(values):
        upper = jnp.concatenate(values[:2], axis=1)
        lower = jnp.concatenate(values[2:], axis=1)
        return jnp.concatenate([upper, lower], axis=0).astype(BF16)

    def unit_copy(k, side):
        return pltpu.make_async_remote_copy(
            src_ref=h_send.at[2 * (k - 1) + side],
            dst_ref=h_buf.at[row, side],
            send_sem=h_sem.at[0, 2 * (k - 1) + side],
            recv_sem=h_sem.at[1, 2 * (k - 1) + side],
            device_id={"row": peer("row", k)},
            device_id_type=MESH,
        )

    if exact:

        @pl.loop(0, 2)
        def _(side):
            for piece in range(4):
                first_part[side, :, piece * chunk : (piece + 1) * chunk] = raw(
                    unit_rows(1, side, piece)
                )

    finish(sq_copies)
    scales = scale_of(total(sq3_buf, n))
    sides = [scales[:, 0:1], scales[:, HD : HD + 1]]
    own_scale = jnp.where(first, sides[0], sides[1])
    factor_c = guidance * my_half(sides[0])
    factor_u = (1.0 - guidance) * my_half(sides[1])

    def blend(logits):
        return factor_c * logits[:half_rows] + factor_u * logits[half_rows:]

    def guided(rows):
        return blend(raw(rows))

    if exact:
        for side in range(2):
            values = [
                blend(first_part[side, :, piece * chunk : (piece + 1) * chunk]) for piece in range(4)
            ]
            h_send[side] = fold(values)
            unit_copy(1, side).start()

        @pl.loop(2, 2 * n)
        def _(unit):
            k = 1 + unit // 2
            side = unit % 2
            folded = fold([guided(unit_rows(k, side, piece)) for piece in range(4)])

            @pl.when(unit < 2 * (n - 1))
            def _():
                h_send[unit] = folded
                unit_copy(k, side).start()

            @pl.when(unit >= 2 * (n - 1))
            def _():
                h_buf[row, side] = folded

    else:
        part[:, whole : part.shape[1]] = jnp.zeros((half_rows, part.shape[1] - whole), F32)
        if whole < vocab:
            part[:, whole:vocab] = guided(wh[whole:vocab, :])
        for k in range(1, n + 1):
            dest = peer("row", k)
            start = dest * share // LANES * LANES
            is_last = (dest + 1) // n
            for piece in range(window // chunk):
                over = max(0, last_start + (piece + 1) * chunk - whole)
                at = pl.multiple_of(start + piece * chunk - is_last * over, LANES)
                part[:, pl.ds(at, chunk)] = guided(wh[pl.ds(at, chunk), :])
            start = pl.multiple_of(start, LANES)
            upper = pl.multiple_of(start + half, LANES)
            stacked = jnp.concatenate(
                [part[:, pl.ds(start, half)], part[:, pl.ds(upper, half)]], axis=0
            )
            if k < n:
                h_send[k - 1] = stacked.astype(BF16)
                copies.append(send(h_send.at[k - 1], h_buf.at[row], "row", 11, k))
            else:
                h_buf[row] = stacked.astype(BF16)

    finish(np_copies)
    sums = own_scale * total(np_buf, n)
    next_ref[...] = sums.astype(BF16)

    if exact:
        for side in range(2):
            for k in range(1, n):
                unit_copy(k, side).wait_recv()
            sums = h_buf[0, side].astype(F32)
            for k in range(1, n):
                sums = sums + h_buf[k, side].astype(F32)
            for quarter in range(2):
                at = side * sub + quarter * 2 * chunk
                wide = min(2 * chunk, share - at)
                top = quarter * half_rows
                out_ref[:, at : at + wide] = sums[top : top + half_rows, 0:wide]
        for side in range(2):
            for k in range(1, n):
                unit_copy(k, side).wait_send()
    else:
        finish(copies)
        sums = total(h_buf, n)
        part[:, 0:half] = sums[:half_rows]
        part[:, half:window] = sums[half_rows:]
        offset = lax.rem(row * share, LANES)
        turn = lax.rem(LANES - offset, LANES)
        lane8 = iota((half_rows, LANES), 1)
        for j in range(-(-share // LANES)):
            here_tile = pltpu.roll(part[:, j * LANES : (j + 1) * LANES], turn, 1)
            next_tile = pltpu.roll(part[:, (j + 1) * LANES : (j + 2) * LANES], turn, 1)
            joined = jnp.where(lane8 < LANES - offset, here_tile, next_tile)
            wide = min(LANES, share - j * LANES)
            out_ref[:, j * LANES : j * LANES + wide] = joined[:, :wide]
    for copy in pending:
        copy.wait_send()


def part_outputs(guided_ref, next_ref, out_ref, query_ref, pairs_ref):
    out_ref[...] = guided_ref[...]
    width_q = query_ref.shape[1]
    width = pairs_ref.shape[2]
    query_ref[...] = next_ref[:, 0:width_q]
    for k in range(2):
        pairs_ref[:, k, :] = next_ref[:, width_q + k * width : width_q + (k + 1) * width]


def local(
    n,
    m,
    hidden,
    lengths,
    kv_cache,
    attn_gain,
    w_query,
    w_key_value,
    w_out,
    mlp_gain,
    w_gate_up,
    w_down,
    final_gain,
    w_head,
    next_gain,
    w_next_query,
    w_next_kv,
    tenant,
    guide_scale,
):
    x_rows = hidden[0]
    requests, width = x_rows.shape
    cache = kv_cache[0]
    head_rows = w_head.T
    weights = (cache, w_query, w_key_value, w_out, w_gate_up, w_down, head_rows, w_next_query, w_next_kv)
    width_q = w_query.shape[1]
    width_kv = 2 * w_key_value.shape[2]
    heads_here = width_q // HD
    hidden_here = w_down.shape[0]
    block = hidden_here // n
    vocab = head_rows.shape[0]
    share = vocab // n
    window = window_of(share)
    last_start = (n - 1) * share // LANES * LANES
    exact = share % SUBLANES == 0 and window % (8 * LANES) == 0
    part_shape = (8, LANES) if exact else (requests // 2, last_start + window)
    held = [a.shape for a in weights]
    if exact:
        held[6] = (vocab + window - share, width)
    first_shape = (2, requests, window // 2) if exact else (requests, LANES)
    scattered = block % LANES == 0
    gu_width = 2 * block if scattered else 2 * hidden_here
    peers = max(n, m) - 1
    vmem = pl.BlockSpec(memory_space=pltpu.VMEM)
    smem = pl.BlockSpec(memory_space=pltpu.SMEM)
    hbm = pl.BlockSpec(memory_space=pl.ANY)
    scratch = [pltpu.VMEM(shape, BF16) for shape in held] + [
        pltpu.VMEM((width, 2 * width), BF16),
        pltpu.VMEM((2 * width, hidden_here), BF16),
        pltpu.VMEM((n, requests, width_q + width_kv), BF16),
        pltpu.VMEM((n, requests, LANES), F32),
        pltpu.VMEM((requests, heads_here, LANES), F32),
        pltpu.VMEM((n, requests, LANES), F32),
        pltpu.VMEM((n, requests, width_q), BF16),
        pltpu.VMEM((m, requests, width), BF16),
        pltpu.VMEM((n, requests, LANES), F32),
        pltpu.VMEM((n - 1 if scattered else 1, requests, gu_width), BF16),
        pltpu.VMEM((n, requests, gu_width), BF16),
        pltpu.VMEM((n, requests, block), BF16),
        pltpu.VMEM((2, m, requests, width), BF16),
        pltpu.VMEM((2, requests, width), BF16),
        pltpu.VMEM((n, requests, LANES), F32),
        pltpu.VMEM((n, requests, width_q + width_kv), BF16),
        pltpu.VMEM(first_shape, F32),
        pltpu.VMEM(part_shape, F32),
        pltpu.VMEM((2 * n - 2, requests, window // 4) if exact else (n - 1, requests, window // 2), BF16),
        pltpu.VMEM((n, 2, requests, window // 4) if exact else (n, requests, window // 2), BF16),
        pltpu.SemaphoreType.DMA((8 + n,)),
        pltpu.SemaphoreType.DMA((14, peers)),
        pltpu.SemaphoreType.DMA((14, peers)),
        pltpu.SemaphoreType.DMA((2, 2, m)),
        pltpu.SemaphoreType.DMA((2, 2 * n)),
    ]
    guided, next_all = pl.pallas_call(
        functools.partial(layer_kernel, n, m),
        out_shape=(
            jax.ShapeDtypeStruct((requests // 2, share), F32),
            jax.ShapeDtypeStruct((requests, width_q + width_kv), BF16),
        ),
        in_specs=[vmem, vmem, vmem, smem] + [vmem] * 4 + [hbm] * 9,
        out_specs=(vmem, vmem),
        scratch_shapes=scratch,
        compiler_params=pltpu.CompilerParams(
            collective_id=0, has_side_effects=True, vmem_limit_bytes=60 * 1024 * 1024
        ),
        name="decode_layer",
    )(x_rows, lengths, tenant.reshape(1, -1), guide_scale, attn_gain, mlp_gain, final_gain, next_gain, *weights)
    guided, next_query, next_pairs = pl.pallas_call(
        part_outputs,
        out_shape=(
            jax.ShapeDtypeStruct(guided.shape, F32),
            jax.ShapeDtypeStruct((requests, width_q), BF16),
            jax.ShapeDtypeStruct((requests, 2, width_kv // 2), BF16),
        ),
        in_specs=[vmem, vmem],
        out_specs=(vmem, vmem, vmem),
        name="part_outputs",
    )(guided, next_all)
    return (guided, next_query[None], next_pairs[None])


def solution(mesh):
    placed = (
        P("guide", None, "row"),
        P("guide", None),
        P("guide", None, None, "row", "col"),
        P("row"),
        P("row", "col"),
        P("row", None, "col"),
        P("col", "row"),
        P("row"),
        P("row", None, "col"),
        P("col", "row"),
        P("row"),
        P("row", "col"),
        P("row"),
        P("row", "col"),
        P("row", None, "col"),
        P(),
        P(),
    )
    return jax.shard_map(
        functools.partial(local, mesh.shape["row"], mesh.shape["col"]),
        mesh=mesh,
        in_specs=placed,
        out_specs=(
            P("guide", ("col", "row")),
            P("guide", None, "col"),
            P("guide", None, None, "col"),
        ),
        check_vma=False,
    )
```
